256 devices in a mesh: blk: 32 (over y_lo, z, core), tensor: 8 (over x, y_hi).
Axes of the slice: x: 4, y: 4 (y_hi: 2, y_lo: 2; y = y_hi * 2 + y_lo), z: 8, core: 2. Of those that a mesh axis runs over, the one named last changes fastest.
Arguments:
- a_query: bfloat16 [16384, 2048], P('blk', 'tensor'), may hold values from -24 to 24
- a_key: bfloat16 [16384, 128], P(('blk', 'tensor')), may hold values from -4 to 4
- a_value: bfloat16 [16384, 128], P(('blk', 'tensor')), may hold values from -6 to 6
- b_query: bfloat16 [1536, 2048], P('blk', 'tensor'), may hold values from -24 to 24
- b_key: bfloat16 [1536, 128], P('blk'), may hold values from -4 to 4
- b_value: bfloat16 [1536, 128], P('blk'), may hold values from -6 to 6
- cache_key: bfloat16 [65536, 128], P(('blk', 'tensor')), may hold values from -4 to 4
- cache_value: bfloat16 [65536, 128], P(('blk', 'tensor')), may hold values from -6 to 6
- a_positions: int32 [16384], replicated, may hold values from 0 to 16383, as said below
- cache_lengths: int32 [32], replicated, may hold values from 1 to 2048, 61440 in all
Outputs:
- a_output: bfloat16 [16384, 2048], P('blk', 'tensor')
- b_output: bfloat16 [1536, 2048], P('blk', 'tensor')
The draws below stay inside these ranges and needn't reach their ends.
Inputs may be any that keep to these rules, and one draw needn't show every extreme that they name: `a_positions`: a permutation of 0 to 16383 made of blocks of 256 consecutive positions in increasing order; the rows of one index of blk hold two blocks, numbers c and 63 - c for some c, in either order.
All inputs are finite; a program needn't handle non-finite values.
Results may differ from the reference program's by a relative error of at most 0.012.
Values may be sent and summed in bfloat16 or wider, within the bound.
A program may use at most 64 MiB of HBM per device.

```python
import math
import jax
import jax.numpy as jnp
import numpy as np
from jax import lax

HD = 128
HEADS = 16
A_DEV = 512
B_DEV = 48
C_DEV = 2048
A_LEN = 16384
B_LEN = 1536
CACHE_LIVE = 61440
N_BLK = 32


def drawn_draw(key, count, heads):
    key_keys, key_query = jax.random.split(key, 2)
    keys = jax.random.randint(key_keys, (count, HD), -12, 13).astype(jnp.float32) * 0.25
    query = jax.random.randint(key_query, (count, heads, HD), -10, 11).astype(jnp.float32) * 0.25
    return (keys, query.reshape(count, heads * HD))


def draw_a_query(key, part):
    return drawn_draw(key, A_LEN, HEADS)[1].astype(jnp.bfloat16)


def draw_a_key(key, part):
    return drawn_draw(key, A_LEN, HEADS)[0].astype(jnp.bfloat16)


def draw_b_query(key, part):
    return drawn_draw(jax.random.fold_in(key, 21), B_LEN, HEADS)[1].astype(jnp.bfloat16)


def draw_b_key(key, part):
    return drawn_draw(jax.random.fold_in(key, 21), B_LEN, HEADS)[0].astype(jnp.bfloat16)


def draw_a_positions(key, part):
    key = jax.random.fold_in(key, 5)
    key_order, key_flip = jax.random.split(key)
    pairs = A_LEN // A_DEV
    order = jax.random.permutation(key_order, pairs)
    flip = jax.random.randint(key_flip, (pairs,), 0, 2)
    higher = 2 * pairs - 1 - order
    first = jnp.where(flip == 1, higher, order)
    second = jnp.where(flip == 1, order, higher)
    blocks = jnp.stack([first, second], axis=1)
    length = A_DEV // 2
    positions = blocks[:, :, None] * length + jnp.arange(length)[None, None, :]
    return positions.reshape(A_LEN).astype(jnp.int32)


def block_levels(own_key, extent, cuts, smallest, high):
    factor_of, own = 1.0, jax.random.fold_in(own_key, 6)
    for axis_at, parts in cuts:
        heights = jnp.exp(jax.random.uniform(jax.random.fold_in(own, axis_at), (parts,), jnp.float32, smallest / len(cuts), high / len(cuts)))
        factor_of = factor_of * jnp.repeat(heights, extent[axis_at] // parts).reshape([-1 if axis == axis_at else 1 for axis in range(len(extent))])
    return factor_of


def profile(number_of, total, most, lean):
    weights = [(1 << 20) // math.isqrt(grade ** lean) + 1 for grade in range(2, number_of + 1)]
    spare, holding = total - most - (number_of - 1), [1] * (number_of - 1)
    while spare > 0:
        candidates = [i for i in range(number_of - 1) if holding[i] < most]
        whole, remaining = sum([weights[i] for i in candidates]), spare
        for i in candidates:
            more = min(most - holding[i], max(1, remaining * weights[i] // whole), spare)
            holding[i] = holding[i] + more
            spare = spare - more
    return np.array([most] + holding)


def ragged_sizes(rng, number_of, total, most, slope):
    if number_of == 2:
        one = jax.random.randint(rng, (), max(1, total - most), min(most, total - 1) + 1)
        return jnp.stack([one, total - one])
    tallies = jnp.asarray(profile(number_of, total, most, slope), jnp.int32)
    pairs = (number_of - 1) // 2
    giver, sink = tallies[1:1 + 2 * pairs:2], tallies[2:2 + 2 * pairs:2]
    room = jnp.minimum(giver - 1, most - sink)
    moved = jax.random.randint(jax.random.fold_in(rng, 1), (pairs,), 0, 1 << 20) % (room + 1)
    tallies = tallies.at[1:1 + 2 * pairs:2].set(giver - moved).at[2:2 + 2 * pairs:2].set(sink + moved)
    return tallies[jax.random.permutation(jax.random.fold_in(rng, 2), number_of)]


def gaussian(own_key, shape, scale, bound, pieces=(), kind=jnp.bfloat16):
    loudness = block_levels(own_key, shape, pieces, -0.22, 0.18) if pieces else 1.0
    values = jax.random.normal(own_key, shape, jnp.float32) * scale * loudness
    return jnp.minimum(jnp.maximum(values, -bound), bound).astype(kind)


def setup_inputs(seed: int = 0) -> dict:
    key_list = jax.random.split(jax.random.key(seed), 11)
    a_query = draw_a_query(jax.random.fold_in(key_list[10], 71), 0)
    a_key = draw_a_key(jax.random.fold_in(key_list[10], 71), 0)
    a_value = gaussian(key_list[2], (A_LEN, HD), 1.0, 6.0, ((0, 256),))
    b_query = draw_b_query(jax.random.fold_in(key_list[10], 71), 0)
    b_key = draw_b_key(jax.random.fold_in(key_list[10], 71), 0)
    b_value = gaussian(key_list[5], (B_LEN, HD), 1.0, 6.0, ((0, 32),))
    cache_key = gaussian(key_list[6], (N_BLK * C_DEV, HD), 1.0, 4.0, ((0, 256),))
    cache_value = gaussian(key_list[7], (N_BLK * C_DEV, HD), 1.0, 6.0, ((0, 256),))
    a_positions = draw_a_positions(jax.random.fold_in(key_list[10], 71), 0)
    cache_lengths = ragged_sizes(key_list[9], N_BLK, CACHE_LIVE, C_DEV, 2).astype(jnp.int32)
    return {"a_query": a_query, "a_key": a_key, "a_value": a_value, "b_query": b_query, "b_key": b_key, "b_value": b_value, "cache_key": cache_key, "cache_value": cache_value, "a_positions": a_positions, "cache_lengths": cache_lengths}


LOWEST = -1e30


def softmax_rows(query_block, query_pos, keys, values, key_pos):
    scores = jnp.dot(query_block, keys.T, preferred_element_type=jnp.float32) * (HD ** -0.5)
    visible = key_pos[None, :] <= query_pos[:, None]
    scores = jnp.where(visible, scores, LOWEST)
    largest = jnp.max(scores, axis=1, keepdims=True)
    weights = jnp.where(visible, jnp.exp(scores - largest), 0.0)
    total = jnp.sum(weights, axis=1, keepdims=True)
    probs = weights.astype(jnp.bfloat16)
    return (jnp.dot(probs, values, preferred_element_type=jnp.float32) / total).astype(jnp.bfloat16)


def attention(query, query_pos, keys, values, key_pos):
    count = query.shape[0]
    block = math.gcd(count, 512)
    blocks = count // block
    per_head = query.reshape(blocks, block, HEADS, HD).transpose(2, 0, 1, 3).reshape(HEADS * blocks, block, HD)
    pos_blocks = jnp.tile(query_pos.reshape(blocks, block), (HEADS, 1))
    result = lax.map(lambda item: softmax_rows(item[0], item[1], keys, values, key_pos), (per_head, pos_blocks))
    return result.reshape(HEADS, blocks, block, HD).transpose(1, 2, 0, 3).reshape(count, HEADS * HD)


def group_partial(b_heads, new_pos, cache_key, cache_value, b_key, b_value, cache_lengths, group):
    start_cache = (group * C_DEV).astype(jnp.int32)
    start_new = (group * B_DEV).astype(jnp.int32)
    keys = jnp.concatenate([lax.dynamic_slice_in_dim(cache_key, start_cache, C_DEV), lax.dynamic_slice_in_dim(b_key, start_new, B_DEV)], axis=0)
    values = jnp.concatenate([lax.dynamic_slice_in_dim(cache_value, start_cache, C_DEV), lax.dynamic_slice_in_dim(b_value, start_new, B_DEV)], axis=0)
    slots = jnp.arange(C_DEV, dtype=jnp.int32)
    limit = lax.dynamic_index_in_dim(cache_lengths, group, 0, keepdims=False)
    cache_pos = jnp.where(slots < limit, -1, B_LEN).astype(jnp.int32)
    key_pos = jnp.concatenate([cache_pos, start_new + jnp.arange(B_DEV, dtype=jnp.int32)], axis=0)
    scores = jnp.einsum("thd,kd->htk", b_heads.astype(jnp.float32), keys.astype(jnp.float32)) * (HD ** -0.5)
    visible = (key_pos[None, :] <= new_pos[:, None])[None]
    scores = jnp.where(visible, scores, LOWEST)
    top = jnp.max(scores, axis=2)
    weights = jnp.where(visible, jnp.exp(scores - top[:, :, None]), 0.0)
    total = jnp.sum(weights, axis=2)
    probs = weights.astype(jnp.bfloat16)
    accum = jnp.einsum("htk,kd->htd", probs.astype(jnp.float32), values.astype(jnp.float32))
    partial_out = (accum / total[:, :, None]).astype(jnp.bfloat16)
    return partial_out, top, total


def reference(a_query, a_key, a_value, b_query, b_key, b_value, cache_key, cache_value, a_positions, cache_lengths):
    a_output = attention(a_query, a_positions, a_key, a_value, a_positions)
    new_pos = jnp.arange(B_LEN, dtype=jnp.int32)
    b_heads = b_query.reshape(B_LEN, HEADS, HD)
    groups = jnp.arange(N_BLK, dtype=jnp.int32)
    partials, tops, totals = lax.map(lambda group: group_partial(b_heads, new_pos, cache_key, cache_value, b_key, b_value, cache_lengths, group), groups)
    best = jnp.max(tops, axis=0)
    share = totals * jnp.exp(tops - best[None])
    numer = jnp.sum(partials.astype(jnp.float32) * share[..., None], axis=0)
    denom = jnp.sum(share, axis=0)
    merged = numer / denom[..., None]
    b_output = merged.transpose(1, 0, 2).reshape(B_LEN, HEADS * HD).astype(jnp.bfloat16)
    return a_output, b_output
```

```python
import functools
import math

import jax
import jax.numpy as jnp
from jax import lax
from jax.experimental import pallas as pl
from jax.experimental.pallas import tpu as pltpu
from jax.sharding import PartitionSpec as P

HD = 128
BLOCK = 256
CHUNK = 4
OWNERS = 4
SCALE2 = HD ** (-0.5) * math.log2(math.e)
LOWEST = -1e30
NT = (((1,), (1,)), ((), ()))
NN = (((1,), (0,)), ((), ()))
MESH = pl.DeviceIdType.MESH


def dot(a, b, dims):
    return lax.dot_general(a, b, dims, preferred_element_type=jnp.float32)


class Copy:
    def __init__(self, book, view, device):
        self.book, self.view, self.device = book, view, device
        self.index = len(book.copies)
        book.copies.append(self)

    def make(self):
        return pltpu.make_async_remote_copy(
            src_ref=self.view(),
            dst_ref=self.view(),
            send_sem=self.book.send.at[self.index],
            recv_sem=self.book.recv.at[self.index],
            device_id=self.device,
            device_id_type=MESH,
        )


class Book:
    def __init__(self, send, recv):
        self.send, self.recv, self.copies = send, recv, []


class Gather:
    def __init__(self, book, views, order, axes, sibling):
        self.steps, self.forwards = [], []
        done = []
        for number, axis in enumerate(order):
            size, at, device = axes[axis]
            final = number == len(order) - 1 and sibling is not None
            if final:
                self.forwards = [[] for step in self.steps]
                self.forwards.append(
                    [Copy(book, v, sibling) for v in views(tuple(done), axis, at, None)]
                )
            for k in range(1, size // 2 + 1):
                sends, arrived = [], []
                for way in (1, -1):
                    if size == 2 and way == -1:
                        continue
                    half = None
                    if 2 * k == size and size > 2:
                        half = 0 if way == 1 else 1
                    out = (at - way * (k - 1) + 2 * size) % size
                    got = (at - way * k + 2 * size) % size
                    for v in views(tuple(done), axis, out, half):
                        sends.append(Copy(book, v, device(way)))
                    if final:
                        for v in views(tuple(done), axis, got, half):
                            arrived.append(Copy(book, v, sibling))
                self.steps.append(sends)
                if final:
                    self.forwards.append(arrived)
            done.append(axis)

    def run(self, step):
        if step > len(self.steps):
            return
        if step > 0:
            for copy in self.steps[step - 1]:
                copy.make().wait_recv()
        if step < len(self.steps):
            for copy in self.steps[step]:
                copy.make().start()
        if step < len(self.forwards):
            for copy in self.forwards[step]:
                copy.make().start()

    def siblings(self):
        for group in self.forwards:
            for copy in group:
                copy.make().wait_recv()


def sizes_of(blocks, heads):
    y_lo, y_hi = 2, 2
    return heads // y_hi, y_hi, y_lo, blocks // (2 * y_lo)


def exchange_kernel(
    blocks,
    heads,
    lengths,
    a_key,
    a_value,
    b_query,
    b_key,
    b_value,
    cache_key,
    cache_value,
    key_x,
    value_y,
    key_z,
    value_z,
    b_out,
    q_all,
    k_all,
    v_all,
    k_buf,
    v_buf,
    column,
    part,
    stat,
    part_in,
    stat_in,
    send,
    recv,
    merge_send,
    merge_recv,
    local,
):
    X, YH, YL, Z = sizes_of(blocks, heads)
    Y = YH * YL
    me, t = lax.axis_index("blk"), lax.axis_index("tensor")
    yl, z, c = me // (2 * Z), (me // 2) % Z, me % 2
    x, yh = t // YH, t % YH
    y = yh * YL + yl

    def dev(x, y, z, c):
        return ((y % YL) * (2 * Z) + z * 2 + c, x * YH + y // YL)

    axes = {
        "x": (X, x, lambda way: dev((x + way + X) % X, y, z, c)),
        "y": (Y, y, lambda way: dev(x, (y + way + Y) % Y, z, c)),
        "z": (Z, z, lambda way: dev(x, y, (z + way + Z) % Z, c)),
        "yl": (YL, yl, lambda way: dev(x, yh * YL + (1 - yl), z, c)),
        "yh": (YH, yh, lambda way: dev(x, (1 - yh) * YL + yl, z, c)),
    }
    sibling = dev(x, y, z, 1 - c)
    every = slice(None)

    def a_views(arrays, lone):
        def views(done, axis, at, half):
            chosen = arrays
            zs = every if "z" in done else (at if axis == "z" else z)
            if half is not None:
                if len(arrays) == 2:
                    chosen = arrays[half:half + 1]
                elif "z" in done:
                    zs = pl.ds(half * (Z // 2), Z // 2)
                elif half != lone:
                    chosen = []
            xs = every if "x" in done else (at if axis == "x" else x)
            if "y" in done:
                yls, yhs = every, every
            elif axis == "y":
                yls, yhs = at % YL, at // YL
            else:
                yls, yhs = yl, yh
            return [lambda a=a: a.at[yls, zs, c, xs, yhs] for a in chosen]

        return views

    def cache_views(done, axis, at, half):
        chosen = [k_all, v_all] if half is None else [k_all, v_all][half:half + 1]
        xs = at if axis == "x" else x
        yhs = every if "yh" in done else (at if axis == "yh" else yh)
        return [lambda a=a: a.at[xs, yhs] for a in chosen]

    def query_views(done, axis, at, half):
        if half == 1:
            return []
        yls = every if "yl" in done else (at if axis == "yl" else yl)
        zs = at if axis == "z" else z
        return [lambda: q_all.at[yls, zs, c]]

    book = Book(send, recv)
    caches = Gather(book, cache_views, ["yh", "x"], axes, None)
    asked = Gather(book, query_views, ["yl", "z"], axes, sibling)
    pieces = [
        Gather(book, a_views([key_x], 0), ["z", "y", "x"], axes, sibling),
        Gather(book, a_views([value_y], 1), ["z", "x", "y"], axes, sibling),
        Gather(book, a_views([key_z, value_z], 0), ["x", "y", "z"], axes, sibling),
    ]

    cut = key_x.shape[5]
    rows = a_key.shape[0]
    locals_ = [
        (cache_key, k_all.at[x, yh]),
        (cache_value, v_all.at[x, yh]),
        (b_query, q_all.at[yl, z, c]),
        (a_key.at[pl.ds(0, cut)], key_x.at[yl, z, c, x, yh]),
        (a_value.at[pl.ds(0, cut)], value_y.at[yl, z, c, x, yh]),
        (a_key.at[pl.ds(cut, rows - cut)], key_z.at[yl, z, c, x, yh]),
        (a_value.at[pl.ds(cut, rows - cut)], value_z.at[yl, z, c, x, yh]),
    ]
    locals_ = [
        pltpu.make_async_copy(a, b, local.at[i]) for i, (a, b) in enumerate(locals_)
    ]
    for copy in locals_:
        copy.start()

    barrier = pltpu.get_barrier_semaphore()
    others = [
        dev((x + 1) % X, y, z, c),
        dev((x + X - 1) % X, y, z, c),
        dev(x, (1 - yh) * YL + yl, z, c),
        dev(x, (1 - yh) * YL + 1 - yl, z, c),
    ]
    if X == 1:
        others = others[2:]
    for other in others:
        pl.semaphore_signal(barrier, inc=1, device_id=other, device_id_type=MESH)

    def greet(r, unused):
        pl.semaphore_signal(
            barrier, inc=1, device_id=((me + r) % blocks, t), device_id_type=MESH
        )
        return unused

    lax.fori_loop(1, blocks, greet, 0)
    pl.semaphore_wait(barrier, len(others) + blocks - 1)
    for copy in locals_:
        copy.wait()

    caches.run(0)
    asked.run(0)
    for piece in pieces:
        piece.run(0)
    column[...] = jnp.zeros(column.shape, jnp.float32)
    fresh = b_key.shape[0]
    count = k_all.shape[0] * k_all.shape[1] * k_all.shape[2]
    early = len(asked.steps)
    for step in range(1, early):
        caches.run(step)
        asked.run(step)
        for piece in pieces:
            piece.run(step)
    for step in range(early, len(caches.steps) + 1):
        caches.run(step)

    live = lax.broadcasted_iota(jnp.int32, (count, HD), 0) < lengths[me]
    keys = k_all[...].reshape(count, HD).astype(jnp.float32)
    values = v_all[...].reshape(count, HD).astype(jnp.float32)
    lead = jnp.broadcast_to(keys[0:1, :], (count, HD))
    k_buf[:count, :] = jnp.where(live, keys, lead).astype(jnp.bfloat16)
    v_buf[:count, :HD] = jnp.where(live, values, 0.0).astype(jnp.bfloat16)
    v_buf[:count, HD:] = jnp.where(live, 1.0, 0.0).astype(jnp.bfloat16)
    k_buf[count:count + fresh, :] = b_key[...]
    k_buf[count + fresh:, :] = jnp.zeros((HD - fresh, HD), jnp.bfloat16)
    v_buf[count:count + fresh, :HD] = b_value[...]
    v_buf[count + fresh:, :HD] = jnp.zeros((HD - fresh, HD), jnp.bfloat16)
    v_buf[count:, HD:] = jnp.ones((HD, HD), jnp.bfloat16)

    asked.run(early)
    asked.siblings()
    tiles = blocks // OWNERS
    tile_rows = OWNERS * fresh
    a_steps = max(len(piece.steps) for piece in pieces)
    late = {early: 0, early + 1: 1, early + 2: 2, early + 3: 6}

    def merge_copies(owner, source, target):
        return [
            pltpu.make_async_remote_copy(
                src_ref=a.at[source],
                dst_ref=b.at[target],
                send_sem=merge_send.at[i, source],
                recv_sem=merge_recv.at[i, target],
                device_id=(owner, t),
                device_id_type=MESH,
            )
            for i, (a, b) in enumerate(((part, part_in), (stat, stat_in)))
        ]

    def own_copies():
        return [
            pltpu.make_async_copy(a.at[me], b.at[me], local.at[i])
            for i, (a, b) in enumerate(((part, part_in), (stat, stat_in)))
        ]

    def tile_step(i, unused):
        for step in range(early, a_steps):
            @pl.when(i == min(late.get(step, tiles - 1), tiles - 1))
            def _():
                for piece in pieces:
                    piece.run(step)

        tile = (me // OWNERS + 1 + i) % tiles
        first = tile * OWNERS
        yl_at, z_at = first // (2 * Z), (first // 2) % Z
        q = q_all[yl_at, pl.ds(z_at, OWNERS // 2)].reshape(tile_rows, 2 * HD)
        bases, sums, outs = [], [], []
        for h in range(2):
            mine = q[:, h * HD:(h + 1) * HD]
            scores = dot(mine, k_buf[:count, :], NT)
            extra = dot(mine, k_buf[count:, :], NT)
            ki = lax.broadcasted_iota(jnp.int32, extra.shape, 1)
            ti = lax.broadcasted_iota(jnp.int32, extra.shape, 0) + first * fresh
            seen = jnp.logical_and(ki < fresh, ki + me * fresh <= ti)
            extra = jnp.where(seen, extra, LOWEST)
            top = jnp.maximum(
                jnp.max(scores, axis=1, keepdims=True), jnp.max(extra, axis=1, keepdims=True)
            )
            base = top * SCALE2
            p = jnp.exp2(scores * SCALE2 - base).astype(jnp.bfloat16)
            p_extra = jnp.exp2(extra * SCALE2 - base).astype(jnp.bfloat16)
            acc = dot(p, v_buf[:count, :], NN) + dot(p_extra, v_buf[count:, :], NN)
            outs.append((acc[:, :HD] / acc[:, HD:]).astype(jnp.bfloat16))
            bases.append(base)
            sums.append(acc[:, HD:HD + 1])
        lane = lax.broadcasted_iota(jnp.int32, (tile_rows, HD), 1)
        packed = jnp.where(
            lane == 0, bases[0], jnp.where(lane == 1, bases[1], jnp.where(lane == 2, sums[0], sums[1]))
        )
        column[:tile_rows, :] = packed
        for j in range(OWNERS):
            for h in range(2):
                part[first + j, :, h * HD:(h + 1) * HD] = outs[h][j * fresh:(j + 1) * fresh]
            stat[first + j] = column[j * fresh:j * fresh + HD, :].T[:8]
        for j in range(OWNERS):
            @pl.when(first + j != me)
            def _():
                for copy in merge_copies(first + j, first + j, me):
                    copy.start()

            @pl.when(first + j == me)
            def _():
                for copy in own_copies():
                    copy.start()

        return unused

    lax.fori_loop(0, tiles, tile_step, 0)
    for piece in pieces:
        piece.run(a_steps)
    for copy in own_copies():
        copy.wait()

    def arrive(r, unused):
        other = (me + r) % blocks
        for copy in merge_copies(other, other, other):
            copy.wait_recv()
        return unused

    lax.fori_loop(1, blocks, arrive, 0)
    for h in range(2):
        base = stat_in[:, h, :]
        best = jnp.max(base, axis=0, keepdims=True)
        share = stat_in[:, 2 + h, :] * jnp.exp2(base - best)
        share = jnp.concatenate(
            [share, jnp.zeros((HD - blocks, HD), jnp.float32)], axis=0
        ).T[:fresh]
        numer = jnp.zeros((fresh, HD), jnp.float32)
        for g in range(blocks):
            numer = numer + share[:, g:g + 1] * part_in[g, :, h * HD:(h + 1) * HD].astype(
                jnp.float32
            )
        denom = jnp.sum(share, axis=1, keepdims=True)
        b_out[:, h * HD:(h + 1) * HD] = (numer / denom).astype(jnp.bfloat16)
    for piece in pieces:
        piece.siblings()
    for copy in book.copies:
        copy.make().wait_send()

    def leave(r, unused):
        other = (me + r) % blocks
        for copy in merge_copies(other, other, other):
            copy.wait_send()
        return unused

    lax.fori_loop(1, blocks, leave, 0)


def exchange(blocks, heads, lengths, a_key, a_value, b_query, b_key, b_value, cache_key, cache_value):
    X, YH, YL, Z = sizes_of(blocks, heads)
    rows = a_key.shape[0]
    cut = rows * 3 // 4
    fresh = b_query.shape[0]
    slots = cache_key.shape[0]
    count = slots * heads

    def whole(height):
        return jax.ShapeDtypeStruct((YL, Z, 2, X, YH, height, HD), jnp.bfloat16)

    anywhere = pl.BlockSpec(memory_space=pl.ANY)
    vmem = pl.BlockSpec(memory_space=pltpu.VMEM)
    copies = 120
    return pl.pallas_call(
        functools.partial(exchange_kernel, blocks, heads),
        out_shape=(
            whole(cut),
            whole(cut),
            whole(rows - cut),
            whole(rows - cut),
            jax.ShapeDtypeStruct(b_query.shape, jnp.bfloat16),
        ),
        in_specs=[pl.BlockSpec(memory_space=pltpu.SMEM)]
        + [anywhere] * 3
        + [vmem] * 2
        + [anywhere] * 2,
        out_specs=[anywhere] * 4 + [vmem],
        scratch_shapes=[
            pltpu.VMEM((YL, Z, 2, fresh, 2 * HD), jnp.bfloat16),
            pltpu.VMEM((X, YH, slots, HD), jnp.bfloat16),
            pltpu.VMEM((X, YH, slots, HD), jnp.bfloat16),
            pltpu.VMEM((count + HD, HD), jnp.bfloat16),
            pltpu.VMEM((count + HD, 2 * HD), jnp.bfloat16),
            pltpu.VMEM((OWNERS * fresh + HD, HD), jnp.float32),
            pltpu.VMEM((blocks, fresh, 2 * HD), jnp.bfloat16),
            pltpu.VMEM((blocks, 8, HD), jnp.float32),
            pltpu.VMEM((blocks, fresh, 2 * HD), jnp.bfloat16),
            pltpu.VMEM((blocks, 8, HD), jnp.float32),
            pltpu.SemaphoreType.DMA((copies,)),
            pltpu.SemaphoreType.DMA((copies,)),
            pltpu.SemaphoreType.DMA((2, blocks)),
            pltpu.SemaphoreType.DMA((2, blocks)),
            pltpu.SemaphoreType.DMA((7,)),
        ],
        compiler_params=pltpu.CompilerParams(
            vmem_limit_bytes=40 * 2**20, collective_id=0, has_side_effects=True
        ),
        cost_estimate=pl.CostEstimate(
            flops=10_000_000_000, bytes_accessed=20_000_000, transcendentals=6_700_000
        ),
        name="exchange",
    )(lengths, a_key, a_value, b_query, b_key, b_value, cache_key, cache_value)


def a_kernel(
    shard_rows, pos_ref, q_ref, kx_ref, vy_ref, kz_ref, vz_ref, o_ref,
    k_buf, v_buf, m_buf, acc_buf, place, sems,
):
    total = kx_ref.shape[0]
    high = kx_ref.shape[1]
    group = lax.axis_index("blk")
    own = [pos_ref[2 * group], pos_ref[2 * group + 1]]
    first = (own[0] + CHUNK) // CHUNK
    steps = (total + CHUNK) // CHUNK

    def invert(i, unused):
        place[pos_ref[i]] = i
        return unused

    lax.fori_loop(0, total, invert, 0)

    def where_at(i):
        part = (i >= first).astype(jnp.int32)
        return part, i - part * first

    def fetch(i):
        part, at = where_at(i)
        slot = i % 2
        for b in range(CHUNK):
            block = place[at * CHUNK + b]
            for source, start, size in ((kx_ref, 0, high), (kz_ref, high, BLOCK - high)):
                pltpu.make_async_copy(
                    source.at[block], k_buf.at[slot, pl.ds(b * BLOCK + start, size)], sems.at[0, slot]
                ).start()
            for source, start, size in ((vy_ref, 0, high), (vz_ref, high, BLOCK - high)):
                pltpu.make_async_copy(
                    source.at[block],
                    v_buf.at[slot, pl.ds(b * BLOCK + start, size), pl.ds(0, HD)],
                    sems.at[1, slot],
                ).start()

    fetch(0)
    v_buf[:, :, HD:] = jnp.ones((2, CHUNK * BLOCK, HD), jnp.bfloat16)
    m_buf[...] = jnp.full(m_buf.shape, LOWEST, jnp.float32)
    acc_buf[...] = jnp.zeros(acc_buf.shape, jnp.float32)

    def step(i, unused):
        part, at = where_at(i)
        mine = jnp.where(part == 1, own[1], own[0])
        slot = i % 2

        @pl.when(i + 1 < steps)
        def _():
            fetch(i + 1)

        pltpu.make_async_copy(k_buf.at[slot], k_buf.at[slot], sems.at[0, slot]).wait()
        halves = v_buf.at[slot, :, pl.ds(0, HD)]
        pltpu.make_async_copy(halves, halves, sems.at[1, slot]).wait()

        def work(masked):
            for h in range(2):
                q = q_ref[pl.ds(pl.multiple_of(part * BLOCK, BLOCK), BLOCK), h * HD:(h + 1) * HD]
                s = dot(q, k_buf[slot], NT)
                if masked:
                    row = lax.broadcasted_iota(jnp.int32, (1, CHUNK * BLOCK), 1)
                    block = row // BLOCK
                    row = row % BLOCK
                    per = shard_rows * 3 // 4
                    rest = shard_rows - per
                    low = row - high
                    early, later = row, per + low
                    for n in range(1, BLOCK // shard_rows):
                        early = early + jnp.where(row >= per * n, rest, 0)
                        later = later + jnp.where(low >= rest * n, per, 0)
                    ki = jnp.where(row < high, early, later) + (block + at * CHUNK - mine) * BLOCK
                    qi = lax.broadcasted_iota(jnp.int32, s.shape, 0)
                    s = jnp.where(ki <= qi, s, LOWEST)
                old = m_buf[part, h]
                new = jnp.maximum(old, jnp.max(s, axis=1, keepdims=True))
                m_buf[part, h] = new
                factor = jnp.exp2((old - new) * SCALE2)
                p = jnp.exp2(s * SCALE2 - new[:, :1] * SCALE2).astype(jnp.bfloat16)
                acc_buf[part, h] = acc_buf[part, h] * factor[:, :1] + dot(p, v_buf[slot], NN)

        last = at == mine // CHUNK

        @pl.when(last)
        def _():
            work(True)

        @pl.when(jnp.logical_not(last))
        def _():
            work(False)

        return unused

    lax.fori_loop(0, steps, step, 0)
    for part in range(2):
        for h in range(2):
            acc = acc_buf[part, h]
            o_ref[part * BLOCK:(part + 1) * BLOCK, h * HD:(h + 1) * HD] = (
                acc[:, :HD] / acc[:, HD:]
            ).astype(jnp.bfloat16)


def attend_a(shard_rows, positions, queries, gathered):
    total = positions.shape[0]
    pieces = [g.reshape(total, -1, HD) for g in gathered]
    return pl.pallas_call(
        functools.partial(a_kernel, shard_rows),
        out_shape=jax.ShapeDtypeStruct(queries.shape, jnp.bfloat16),
        grid_spec=pltpu.PrefetchScalarGridSpec(
            num_scalar_prefetch=1,
            grid=(1,),
            in_specs=[pl.BlockSpec(queries.shape, lambda i, p: (0, 0))]
            + [pl.BlockSpec(memory_space=pl.ANY)] * 4,
            out_specs=pl.BlockSpec(queries.shape, lambda i, p: (0, 0)),
            scratch_shapes=[
                pltpu.VMEM((2, CHUNK * BLOCK, HD), jnp.bfloat16),
                pltpu.VMEM((2, CHUNK * BLOCK, 2 * HD), jnp.bfloat16),
                pltpu.VMEM((2, 2, BLOCK, HD), jnp.float32),
                pltpu.VMEM((2, 2, BLOCK, 2 * HD), jnp.float32),
                pltpu.SMEM((total,), jnp.int32),
                pltpu.SemaphoreType.DMA((2, 2)),
            ],
        ),
        compiler_params=pltpu.CompilerParams(vmem_limit_bytes=40 * 2**20),
        cost_estimate=pl.CostEstimate(
            flops=10_000_000_000, bytes_accessed=9_000_000, transcendentals=8_500_000
        ),
        name="attend_a",
    )(positions, queries, *pieces)


def shards(
    blocks,
    heads,
    a_query,
    a_key,
    a_value,
    b_query,
    b_key,
    b_value,
    cache_key,
    cache_value,
    a_positions,
    cache_lengths,
):
    *gathered, b_output = exchange(
        blocks, heads, cache_lengths, a_key, a_value, b_query, b_key, b_value, cache_key, cache_value
    )
    order = lax.slice(a_positions, (0,), a_positions.shape, (BLOCK,)) // BLOCK
    a_output = attend_a(a_key.shape[0], order, a_query, gathered)
    return (a_output, b_output)


def solution(mesh):
    in_specs = (
        P("blk", "tensor"),
        P(("blk", "tensor"), None),
        P(("blk", "tensor"), None),
        P("blk", "tensor"),
        P("blk", None),
        P("blk", None),
        P(("blk", "tensor"), None),
        P(("blk", "tensor"), None),
        P(),
        P(),
    )
    out_specs = (P("blk", "tensor"), P("blk", "tensor"))
    body = functools.partial(shards, mesh.shape["blk"], mesh.shape["tensor"])
    return jax.shard_map(body, mesh=mesh, in_specs=in_specs, out_specs=out_specs, check_vma=False)
```

```python
import functools
import math

import jax
import jax.numpy as jnp
from jax import lax
from jax.experimental import pallas as pl
from jax.experimental.pallas import tpu as pltpu
from jax.sharding import PartitionSpec as P

HD = 128
BLOCK = 256
CHUNK = 4
OWNERS = 4
SCALE2 = HD ** (-0.5) * math.log2(math.e)
LOWEST = -1e30
NT = (((1,), (1,)), ((), ()))
NN = (((1,), (0,)), ((), ()))
MESH = pl.DeviceIdType.MESH


def dot(a, b, dims):
    return lax.dot_general(a, b, dims, preferred_element_type=jnp.float32)


class Copy:
    def __init__(self, book, view, device):
        self.book, self.view, self.device = book, view, device
        self.index = len(book.copies)
        book.copies.append(self)

    def make(self):
        return pltpu.make_async_remote_copy(
            src_ref=self.view(),
            dst_ref=self.view(),
            send_sem=self.book.send.at[self.index],
            recv_sem=self.book.recv.at[self.index],
            device_id=self.device,
            device_id_type=MESH,
        )


class Book:
    def __init__(self, send, recv):
        self.send, self.recv, self.copies = send, recv, []


class Gather:
    def __init__(self, book, views, order, axes, sibling):
        self.steps, self.forwards = [], []
        done = []
        for number, name in enumerate(order):
            axis = name.rstrip("*")
            size, at, device = axes[axis]
            final = number == len(order) - 1 and sibling is not None
            if final:
                self.forwards = [[] for step in self.steps]
                self.forwards.append(
                    [Copy(book, v, sibling) for v in views(tuple(done), axis, at, None)]
                )
            if name.endswith("*"):
                sends = []
                for way in range(1, size):
                    for v in views(tuple(done), axis, at, None):
                        sends.append(Copy(book, v, device(way)))
                if sends:
                    self.steps.append(sends)
                done.append(axis)
                continue
            for k in range(1, size // 2 + 1):
                sends, arrived = [], []
                for way in (1, -1):
                    if size == 2 and way == -1:
                        continue
                    half = None
                    if 2 * k == size and size > 2:
                        half = 0 if way == 1 else 1
                    out = (at - way * (k - 1) + 2 * size) % size
                    got = (at - way * k + 2 * size) % size
                    for v in views(tuple(done), axis, out, half):
                        sends.append(Copy(book, v, device(way)))
                    if final:
                        for v in views(tuple(done), axis, got, half):
                            arrived.append(Copy(book, v, sibling))
                self.steps.append(sends)
                if final:
                    self.forwards.append(arrived)
            done.append(axis)

    def run(self, step):
        if step > len(self.steps):
            return
        if step > 0:
            for copy in self.steps[step - 1]:
                copy.make().wait_recv()
        if step < len(self.steps):
            for copy in self.steps[step]:
                copy.make().start()
        if step < len(self.forwards):
            for copy in self.forwards[step]:
                copy.make().start()

    def siblings(self):
        for group in self.forwards:
            for copy in group:
                copy.make().wait_recv()


def sizes_of(blocks, heads):
    y_lo, y_hi = 2, 2
    return heads // y_hi, y_hi, y_lo, blocks // (2 * y_lo)


def exchange_kernel(
    blocks,
    heads,
    lengths_hbm,
    positions_hbm,
    a_key,
    a_value,
    b_query,
    b_key,
    b_value,
    cache_key,
    cache_value,
    key_all,
    value_all,
    part_in,
    stat_in,
    order,
    lengths,
    positions,
    q_all,
    k_all,
    v_all,
    k_buf,
    v_buf,
    part,
    col,
    part_near,
    col_near,
    held,
    held_col,
    column,
    part_out,
    stat_out,
    send,
    recv,
    near_send,
    near_recv,
    merge_send,
    merge_recv,
    local,
):
    X, YH, YL, Z = sizes_of(blocks, heads)
    Y = YH * YL
    me, t = lax.axis_index("blk"), lax.axis_index("tensor")
    yl, z, c = me // (2 * Z), (me // 2) % Z, me % 2
    x, yh = t // YH, t % YH
    y = yh * YL + yl
    mine = yl * Z + z
    chips = YL * Z

    def dev(x, y, z, c):
        return ((y % YL) * (2 * Z) + z * 2 + c, x * YH + y // YL)

    axes = {
        "x": (X, x, lambda way: dev((x + way + X) % X, y, z, c)),
        "y": (Y, y, lambda way: dev(x, (y + way + Y) % Y, z, c)),
        "z": (Z, z, lambda way: dev(x, y, (z + way + Z) % Z, c)),
        "yl": (YL, yl, lambda way: dev(x, yh * YL + (1 - yl), z, c)),
        "yh": (YH, yh, lambda way: dev(x, (1 - yh) * YL + yl, z, c)),
    }
    sibling = dev(x, y, z, 1 - c)
    every = slice(None)
    rows = a_key.shape[0]
    cut = rows * 3 // 4
    upper, lower = pl.ds(0, cut), pl.ds(cut, rows - cut)

    def a_views(arrays, lone):
        def views(done, axis, at, half):
            chosen = arrays
            zs = every if "z" in done else (at if axis == "z" else z)
            if half is not None:
                if len(arrays) == 2:
                    chosen = arrays[half:half + 1]
                elif "z" in done:
                    zs = pl.ds(half * (Z // 2), Z // 2)
                elif half != lone:
                    chosen = []
            xs = every if "x" in done else (at if axis == "x" else x)
            if "y" in done:
                yls, yhs = every, every
            elif axis == "y":
                yls, yhs = at % YL, at // YL
            else:
                yls, yhs = yl, yh
            return [lambda a=a, r=r: a.at[yls, zs, c, xs, yhs, r] for a, r in chosen]

        return views

    def near_views(done, axis, at, half):
        chosen = [k_all, v_all] if half is None else [k_all, v_all][half:half + 1]
        return [lambda a=a: a.at[yh, at] for a in chosen]

    def far_views(done, axis, at, half):
        chosen = [k_all, v_all] if half is None else [k_all, v_all][half:half + 1]
        if axis == "yh":
            return [lambda a=a: a.at[at, x] for a in chosen]
        return [lambda a=a: a.at[1 - yh, at] for a in chosen]

    def query_views(done, axis, at, half):
        if half == 1:
            return []
        yls = every if "yl" in done else (at if axis == "yl" else yl)
        zs = at if axis == "z" else z
        return [lambda: q_all.at[yls, zs, c]]

    book = Book(send, recv)
    near = Gather(book, near_views, ["x"], axes, None)
    far = Gather(book, far_views, ["yh", "x"], axes, None)
    asked = Gather(book, query_views, ["yl", "z"], axes, sibling)
    piece_x = Gather(book, a_views([(key_all, upper)], 0), ["z*", "y", "x"], axes, sibling)
    piece_y = Gather(book, a_views([(value_all, upper)], 1), ["z*", "x", "y"], axes, sibling)
    piece_z = Gather(
        book, a_views([(key_all, lower), (value_all, lower)], 0), ["x*", "y*", "z"], axes, sibling
    )

    fresh = b_query.shape[0]
    count = k_all.shape[1] * k_all.shape[2]
    locals_ = [
        (cache_key, k_all.at[yh, x]),
        (cache_value, v_all.at[yh, x]),
        (b_query, q_all.at[yl, z, c]),
        (a_key, key_all.at[yl, z, c, x, yh]),
        (a_value, value_all.at[yl, z, c, x, yh]),
        (b_key, k_buf.at[pl.ds(count, fresh)]),
        (b_value, v_buf.at[pl.ds(count, fresh), pl.ds(0, HD)]),
        (lengths_hbm, lengths),
        (positions_hbm, positions),
    ]
    locals_ = [
        pltpu.make_async_copy(a, b, local.at[i]) for i, (a, b) in enumerate(locals_)
    ]
    for copy in locals_:
        copy.start()

    barrier = pltpu.get_barrier_semaphore()
    others = [dev((x + r) % X, y, z, c) for r in range(1, X)] + [
        dev(x, (1 - yh) * YL + yl, z, c),
        dev(x, (1 - yh) * YL + 1 - yl, z, c),
        sibling,
    ]
    for other in others:
        pl.semaphore_signal(barrier, inc=1, device_id=other, device_id_type=MESH)

    def greet(r, unused):
        pl.semaphore_signal(
            barrier, inc=1, device_id=((me + 2 * r) % blocks, t), device_id_type=MESH
        )
        return unused

    lax.fori_loop(1, chips, greet, 0)
    pl.semaphore_wait(barrier, len(others) + chips - 1)
    for copy in locals_:
        copy.wait()

    far.run(0)
    near.run(0)
    asked.run(0)
    piece_z.run(0)
    piece_x.run(0)
    piece_y.run(0)
    column[...] = jnp.zeros(column.shape, jnp.float32)
    k_buf[count + fresh:, :] = jnp.zeros((HD - fresh, HD), jnp.bfloat16)
    v_buf[count + fresh:, :HD] = jnp.zeros((HD - fresh, HD), jnp.bfloat16)
    v_buf[count:, HD:] = jnp.ones((HD, HD), jnp.bfloat16)
    asked.run(1)
    asked.run(2)
    near.run(1)
    piece_z.run(1)
    piece_x.run(1)
    piece_y.run(1)
    asked.run(3)
    far.run(1)
    piece_z.run(2)
    asked.run(4)
    near.run(2)

    def label(i, unused):
        order[i] = positions[i * BLOCK] // BLOCK
        return unused

    lax.fori_loop(0, order.shape[0], label, 0)
    slots = k_all.shape[2]
    side = X * slots
    limit = lengths[me]

    def prepare(which, lead):
        row = lax.broadcasted_iota(jnp.int32, (side, HD), 0)
        live = (row // slots) * (YH * slots) + row % slots + which * slots < limit
        keys = k_all[which].reshape(side, HD).astype(jnp.float32)
        values = v_all[which].reshape(side, HD).astype(jnp.float32)
        lead = jnp.broadcast_to(lead, (side, HD))
        k_buf[:side, :] = jnp.where(live, keys, lead).astype(jnp.bfloat16)
        v_buf[:side, :HD] = jnp.where(live, values, 0.0).astype(jnp.bfloat16)
        v_buf[:side, HD:] = jnp.where(live, 1.0, 0.0).astype(jnp.bfloat16)

    prepare(yh, k_all[yh, 0][:1].astype(jnp.float32))
    piece_x.run(2)
    piece_y.run(2)
    asked.run(5)
    asked.siblings()

    tiles = blocks // OWNERS
    zs_tile = OWNERS // 2
    tile_rows = OWNERS * fresh
    late = [
        (0, piece_z, 4), (2, piece_z, 5), (4, piece_x, 4), (4, piece_y, 4), (6, piece_z, 6),
    ]
    soon = [(1, far, 2), (3, piece_x, 3), (3, piece_y, 3), (4, piece_z, 3)]

    def tile_of(i):
        first = ((me // OWNERS + 1 + i) % tiles) * OWNERS
        return first, first // (2 * Z), (first // 2) % Z

    def near_copies(i):
        return [
            pltpu.make_async_remote_copy(
                src_ref=a.at[i, 1 - c],
                dst_ref=b.at[i],
                send_sem=near_send.at[n, i],
                recv_sem=near_recv.at[n, i],
                device_id=sibling,
                device_id_type=MESH,
            )
            for n, (a, b) in enumerate(((part, part_near), (col, col_near)))
        ]

    def merge_copies(source, slot, owner, sem):
        return [
            pltpu.make_async_remote_copy(
                src_ref=a.at[source],
                dst_ref=b.at[slot],
                send_sem=merge_send.at[n, sem],
                recv_sem=merge_recv.at[n, slot],
                device_id=(owner, t),
                device_id_type=MESH,
            )
            for n, (a, b) in enumerate(((part_out, part_in), (stat_out, stat_in)))
        ]

    def own_copies(source):
        return [
            pltpu.make_async_copy(a.at[source], b.at[mine], local.at[n])
            for n, (a, b) in enumerate(((part_out, part_in), (stat_out, stat_in)))
        ]

    lane = lax.broadcasted_iota(jnp.int32, (fresh, HD), 1)

    def finish(i):
        for copy in near_copies(i):
            copy.wait_recv()
        first, yl_at, z_at = tile_of(i)
        for n in range(zs_tile):
            ours, theirs = col[i, c, n], col_near[i, n]
            stats = []
            for h in range(2):
                base0, base1 = ours[:, h:h + 1], theirs[:, h:h + 1]
                base = jnp.maximum(base0, base1)
                share0 = ours[:, 2 + h:3 + h] * jnp.exp2(base0 - base)
                share1 = theirs[:, 2 + h:3 + h] * jnp.exp2(base1 - base)
                total = share0 + share1
                at = slice(h * HD, (h + 1) * HD)
                both = share0 * part[i, c, n, :, at].astype(jnp.float32) + share1 * part_near[
                    i, n, :, at
                ].astype(jnp.float32)
                part_out[zs_tile * i + n, :, at] = (both / total).astype(jnp.bfloat16)
                stats += [base, total]
            column[:fresh, :] = jnp.where(
                lane == 0,
                stats[0],
                jnp.where(lane == 1, stats[2], jnp.where(lane == 2, stats[1], stats[3])),
            )
            stat_out[zs_tile * i + n] = column[...].T[:8]
        for n in range(zs_tile):
            owner = first + 2 * n + c
            slot = yl_at * Z + z_at + n

            @pl.when(owner != me)
            def _():
                for copy in merge_copies(zs_tile * i + n, mine, owner, slot):
                    copy.start()

            @pl.when(owner == me)
            def _():
                for copy in own_copies(zs_tile * i + n):
                    copy.start()

    wide = lax.broadcasted_iota(jnp.int32, (tile_rows, HD), 1)

    def pack(bases, sums):
        return jnp.where(
            wide == 0, bases[0], jnp.where(wide == 1, bases[1], jnp.where(wide == 2, sums[0], sums[1]))
        )

    def near_step(i, unused):
        for at, piece, step in soon:
            @pl.when(i == min(at, tiles - 1))
            def _():
                piece.run(step)

        first, yl_at, z_at = tile_of(i)
        q = q_all[yl_at, pl.ds(z_at, zs_tile)].reshape(tile_rows, 2 * HD)
        bases, sums = [], []
        for h in range(2):
            scores = dot(q[:, h * HD:(h + 1) * HD], k_buf[:side, :], NT)
            base = jnp.max(scores, axis=1, keepdims=True) * SCALE2
            p = jnp.exp2(scores * SCALE2 - base).astype(jnp.bfloat16)
            acc = dot(p, v_buf[:side, :], NN)
            held[i, :, h * HD:(h + 1) * HD] = acc[:, :HD]
            bases.append(jnp.where(yh * slots < limit, base, LOWEST))
            sums.append(acc[:, HD:HD + 1])
        held_col[i] = pack(bases, sums)
        return unused

    lax.fori_loop(0, tiles, near_step, 0)
    far.run(3)
    prepare(1 - yh, k_all[0, 0][:1].astype(jnp.float32))

    def tile_step(i, unused):
        for at, piece, step in late:
            @pl.when(i == min(at, tiles - 1))
            def _():
                piece.run(step)

        first, yl_at, z_at = tile_of(i)
        q = q_all[yl_at, pl.ds(z_at, zs_tile)].reshape(tile_rows, 2 * HD)
        before = held_col[i]
        bases, sums, outs = [], [], []
        for h in range(2):
            mine_q = q[:, h * HD:(h + 1) * HD]
            scores = dot(mine_q, k_buf[:side, :], NT)
            extra = dot(mine_q, k_buf[side:, :], NT)
            ki = lax.broadcasted_iota(jnp.int32, extra.shape, 1)
            ti = lax.broadcasted_iota(jnp.int32, extra.shape, 0) + first * fresh
            seen = jnp.logical_and(ki < fresh, ki + me * fresh <= ti)
            extra = jnp.where(seen, extra, LOWEST)
            top = jnp.maximum(
                jnp.max(scores, axis=1, keepdims=True), jnp.max(extra, axis=1, keepdims=True)
            )
            old = before[:, h:h + 1]
            base = jnp.maximum(old, top * SCALE2)
            factor = jnp.exp2(old - base)
            p = jnp.exp2(scores * SCALE2 - base).astype(jnp.bfloat16)
            p_extra = jnp.exp2(extra * SCALE2 - base).astype(jnp.bfloat16)
            acc = dot(p, v_buf[:side, :], NN) + dot(p_extra, v_buf[side:, :], NN)
            total = acc[:, HD:HD + 1] + before[:, 2 + h:3 + h] * factor
            outs.append(
                ((acc[:, :HD] + held[i, :, h * HD:(h + 1) * HD] * factor) / total).astype(
                    jnp.bfloat16
                )
            )
            bases.append(base)
            sums.append(total)
        packed = pack(bases, sums)
        for j in range(OWNERS):
            at = slice(j * fresh, (j + 1) * fresh)
            for h in range(2):
                part[i, j % 2, j // 2, :, h * HD:(h + 1) * HD] = outs[h][at]
            col[i, j % 2, j // 2] = packed[at]
        for copy in near_copies(i):
            copy.start()

        @pl.when(i > 0)
        def _():
            finish(i - 1)

        return unused

    lax.fori_loop(0, tiles, tile_step, 0)
    finish(tiles - 1)
    piece_x.run(5)
    piece_y.run(5)
    for copy in own_copies(0):
        copy.wait()

    def arrive(r, unused):
        other = (mine + r) % chips
        for copy in merge_copies(0, other, 2 * other + c, other):
            copy.wait_recv()
        return unused

    lax.fori_loop(1, chips, arrive, 0)
    for piece in (piece_x, piece_y, piece_z):
        piece.siblings()
    for copy in book.copies:
        copy.make().wait_send()

    def leave(r, unused):
        other = (mine + r) % chips
        for copy in merge_copies(0, other, 2 * other + c, other):
            copy.wait_send()
        return unused

    lax.fori_loop(1, chips, leave, 0)

    def part_ways(i, unused):
        for copy in near_copies(i):
            copy.wait_send()
        return unused

    lax.fori_loop(0, tiles, part_ways, 0)


def exchange(blocks, heads, lengths, positions, a_key, a_value, b_query, b_key, b_value, cache_key, cache_value):
    X, YH, YL, Z = sizes_of(blocks, heads)
    rows = a_key.shape[0]
    fresh = b_query.shape[0]
    slots = cache_key.shape[0]
    count = slots * X
    chips = YL * Z
    tiles = blocks // OWNERS
    half = OWNERS // 2
    whole = jax.ShapeDtypeStruct((YL, Z, 2, X, YH, rows, HD), jnp.bfloat16)
    hbm = pl.BlockSpec(memory_space=pltpu.HBM)
    anywhere = pl.BlockSpec(memory_space=pl.ANY)
    copies = 128
    return pl.pallas_call(
        functools.partial(exchange_kernel, blocks, heads),
        out_shape=(
            whole,
            whole,
            jax.ShapeDtypeStruct((chips, fresh, 2 * HD), jnp.bfloat16),
            jax.ShapeDtypeStruct((chips, 8, HD), jnp.float32),
            jax.ShapeDtypeStruct((positions.shape[0] // BLOCK,), jnp.int32),
        ),
        in_specs=[hbm] * 9,
        out_specs=[anywhere] * 4 + [pl.BlockSpec(memory_space=pltpu.SMEM)],
        scratch_shapes=[
            pltpu.SMEM(lengths.shape, jnp.int32),
            pltpu.SMEM(positions.shape, jnp.int32),
            pltpu.VMEM((YL, Z, 2, fresh, 2 * HD), jnp.bfloat16),
            pltpu.VMEM((YH, X, slots, HD), jnp.bfloat16),
            pltpu.VMEM((YH, X, slots, HD), jnp.bfloat16),
            pltpu.VMEM((count + HD, HD), jnp.bfloat16),
            pltpu.VMEM((count + HD, 2 * HD), jnp.bfloat16),
            pltpu.VMEM((tiles, 2, half, fresh, 2 * HD), jnp.bfloat16),
            pltpu.VMEM((tiles, 2, half, fresh, HD), jnp.float32),
            pltpu.VMEM((tiles, half, fresh, 2 * HD), jnp.bfloat16),
            pltpu.VMEM((tiles, half, fresh, HD), jnp.float32),
            pltpu.VMEM((tiles, OWNERS * fresh, 2 * HD), jnp.float32),
            pltpu.VMEM((tiles, OWNERS * fresh, HD), jnp.float32),
            pltpu.VMEM((HD, HD), jnp.float32),
            pltpu.VMEM((chips, fresh, 2 * HD), jnp.bfloat16),
            pltpu.VMEM((chips, 8, HD), jnp.float32),
            pltpu.SemaphoreType.DMA((copies,)),
            pltpu.SemaphoreType.DMA((copies,)),
            pltpu.SemaphoreType.DMA((2, tiles)),
            pltpu.SemaphoreType.DMA((2, tiles)),
            pltpu.SemaphoreType.DMA((2, chips)),
            pltpu.SemaphoreType.DMA((2, chips)),
            pltpu.SemaphoreType.DMA((9,)),
        ],
        compiler_params=pltpu.CompilerParams(
            vmem_limit_bytes=32 * 2**20, collective_id=0, has_side_effects=True
        ),
        cost_estimate=pl.CostEstimate(
            flops=10_000_000_000, bytes_accessed=20_000_000, transcendentals=6_700_000
        ),
        name="exchange",
    )(
        *[
            pltpu.with_memory_space_constraint(v, pltpu.HBM)
            for v in (
                lengths, positions, a_key, a_value, b_query, b_key, b_value, cache_key, cache_value
            )
        ]
    )


def a_kernel(
    fresh, pos_ref, q_ref, key_ref, value_ref, part_ref, stat_ref, o_ref, b_ref,
    q_buf, m_buf, acc_buf, place,
):
    total = key_ref.shape[0]
    chips = part_ref.shape[0]
    group = lax.axis_index("blk")
    own = [pos_ref[2 * group], pos_ref[2 * group + 1]]
    wholes = own[0] // CHUNK
    steps = total // CHUNK - 1
    unroll = 3 if steps % 3 == 0 else 1

    def invert(i, unused):
        place[pos_ref[i]] = i
        return unused

    lax.fori_loop(0, total, invert, 0)
    ones = jnp.ones((CHUNK * BLOCK, HD), jnp.bfloat16)
    for part in range(2):
        for h in range(2):
            q = q_ref[part * BLOCK:(part + 1) * BLOCK, h * HD:(h + 1) * HD]
            q = q.astype(jnp.float32) * SCALE2
            main = q.astype(jnp.bfloat16)
            q_buf[part, h, :, :HD] = main
            q_buf[part, h, :, HD:] = (q - main.astype(jnp.float32)).astype(jnp.bfloat16)

    def load(at):
        where = [place[at * CHUNK + b] for b in range(CHUNK)]
        keys = jnp.concatenate([key_ref[w] for w in where], axis=0)
        values = jnp.concatenate([value_ref[w] for w in where], axis=0)
        return jnp.concatenate([keys, keys], axis=1), jnp.concatenate([values, ones], axis=1)

    for part in range(2):
        at = own[part] // CHUNK
        keys, values = load(at)
        for h in range(2):
            s = dot(q_buf[part, h], keys, NT)
            ki = lax.broadcasted_iota(jnp.int32, s.shape, 1) + (at * CHUNK - own[part]) * BLOCK
            qi = lax.broadcasted_iota(jnp.int32, s.shape, 0)
            s = jnp.where(ki <= qi, s, LOWEST)
            new = jnp.max(s, axis=1, keepdims=True)
            m_buf[part, h] = jnp.broadcast_to(new, (BLOCK, HD))
            p = jnp.exp2(s - new).astype(jnp.bfloat16)
            acc_buf[part, h] = dot(p, values, NN)

    def step(j, unused):
        for n in range(unroll):
            i = j * unroll + n
            part = (i >= wholes).astype(jnp.int32)
            keys, values = load(i - part * wholes)
            for h in range(2):
                s = dot(q_buf[part, h], keys, NT)
                old = m_buf[part, h]
                new = jnp.maximum(old, jnp.max(s, axis=1, keepdims=True))
                m_buf[part, h] = new
                factor = jnp.exp2(old - new)
                p = jnp.exp2(s - new[:, :1]).astype(jnp.bfloat16)
                acc_buf[part, h] = acc_buf[part, h] * factor[:, :1] + dot(p, values, NN)
        return unused

    lax.fori_loop(0, steps // unroll, step, 0)
    for part in range(2):
        for h in range(2):
            acc = acc_buf[part, h]
            o_ref[part * BLOCK:(part + 1) * BLOCK, h * HD:(h + 1) * HD] = (
                acc[:, :HD] / acc[:, HD:]
            ).astype(jnp.bfloat16)

    for h in range(2):
        base = stat_ref[:, h, :]
        best = jnp.max(base, axis=0, keepdims=True)
        share = stat_ref[:, 2 + h, :] * jnp.exp2(base - best)
        share = jnp.concatenate(
            [share, jnp.zeros((HD - chips, HD), jnp.float32)], axis=0
        ).T[:fresh]
        numer = jnp.zeros((fresh, HD), jnp.float32)
        for g in range(chips):
            numer = numer + share[:, g:g + 1] * part_ref[g, :, h * HD:(h + 1) * HD].astype(
                jnp.float32
            )
        denom = jnp.sum(share, axis=1, keepdims=True)
        b_ref[:, h * HD:(h + 1) * HD] = (numer / denom).astype(jnp.bfloat16)


def attend_a(fresh, positions, queries, keys, values, part, stat):
    total = positions.shape[0]
    vmem = pl.BlockSpec(memory_space=pltpu.VMEM)
    return pl.pallas_call(
        functools.partial(a_kernel, fresh),
        out_shape=(
            jax.ShapeDtypeStruct(queries.shape, jnp.bfloat16),
            jax.ShapeDtypeStruct((fresh, 2 * HD), jnp.bfloat16),
        ),
        in_specs=[pl.BlockSpec(memory_space=pltpu.SMEM)] + [vmem] * 5,
        out_specs=[vmem, vmem],
        scratch_shapes=[
            pltpu.VMEM((2, 2, BLOCK, 2 * HD), jnp.bfloat16),
            pltpu.VMEM((2, 2, BLOCK, HD), jnp.float32),
            pltpu.VMEM((2, 2, BLOCK, 2 * HD), jnp.float32),
            pltpu.SMEM((total,), jnp.int32),
        ],
        compiler_params=pltpu.CompilerParams(vmem_limit_bytes=32 * 2**20),
        cost_estimate=pl.CostEstimate(
            flops=10_000_000_000, bytes_accessed=9_000_000, transcendentals=8_500_000
        ),
        name="attend_a",
    )(positions, queries, keys.reshape(total, -1, HD), values.reshape(total, -1, HD), part, stat)


def shards(
    blocks,
    heads,
    a_query,
    a_key,
    a_value,
    b_query,
    b_key,
    b_value,
    cache_key,
    cache_value,
    a_positions,
    cache_lengths,
):
    *gathered, order = exchange(
        blocks,
        heads,
        cache_lengths,
        a_positions,
        a_key,
        a_value,
        b_query,
        b_key,
        b_value,
        cache_key,
        cache_value,
    )
    return attend_a(b_query.shape[0], order, a_query, *gathered)


def solution(mesh):
    in_specs = (
        P("blk", "tensor"),
        P(("blk", "tensor"), None),
        P(("blk", "tensor"), None),
        P("blk", "tensor"),
        P("blk", None),
        P("blk", None),
        P(("blk", "tensor"), None),
        P(("blk", "tensor"), None),
        P(),
        P(),
    )
    out_specs = (P("blk", "tensor"), P("blk", "tensor"))
    body = functools.partial(shards, mesh.shape["blk"], mesh.shape["tensor"])
    return jax.shard_map(body, mesh=mesh, in_specs=in_specs, out_specs=out_specs, check_vma=False)
```

```python
import functools
import math

import jax
import jax.numpy as jnp
from jax import lax
from jax.experimental import pallas as pl
from jax.experimental.pallas import tpu as pltpu
from jax.sharding import PartitionSpec as P

HD = 128
BLOCK = 256
CHUNK = 4
OWNERS = 4
SCALE2 = HD ** (-0.5) * math.log2(math.e)
LOWEST = -1e30
NT = (((1,), (1,)), ((), ()))
NN = (((1,), (0,)), ((), ()))
MESH = pl.DeviceIdType.MESH


def dot(a, b, dims):
    return lax.dot_general(a, b, dims, preferred_element_type=jnp.float32)


class Copy:
    def __init__(self, book, view, device):
        self.book, self.view, self.device = book, view, device
        self.index = len(book.copies)
        book.copies.append(self)

    def make(self):
        return pltpu.make_async_remote_copy(
            src_ref=self.view(),
            dst_ref=self.view(),
            send_sem=self.book.send.at[self.index],
            recv_sem=self.book.recv.at[self.index],
            device_id=self.device,
            device_id_type=MESH,
        )


class Book:
    def __init__(self, send, recv):
        self.send, self.recv, self.copies = send, recv, []


class Gather:
    def __init__(self, book, views, order, axes, sibling):
        self.steps, self.forwards = [], []
        done = []
        for number, name in enumerate(order):
            axis = name.rstrip("*")
            size, at, device = axes[axis]
            final = number == len(order) - 1 and sibling is not None
            if final:
                self.forwards = [[] for step in self.steps]
                self.forwards.append(
                    [Copy(book, v, sibling) for v in views(tuple(done), axis, at, None)]
                )
            if name.endswith("*"):
                sends = []
                for way in range(1, size):
                    for v in views(tuple(done), axis, at, None):
                        sends.append(Copy(book, v, device(way)))
                if sends:
                    self.steps.append(sends)
                done.append(axis)
                continue
            for k in range(1, size // 2 + 1):
                sends, arrived = [], []
                for way in (1, -1):
                    if size == 2 and way == -1:
                        continue
                    half = None
                    if 2 * k == size and size > 2:
                        half = 0 if way == 1 else 1
                    out = (at - way * (k - 1) + 2 * size) % size
                    got = (at - way * k + 2 * size) % size
                    for v in views(tuple(done), axis, out, half):
                        sends.append(Copy(book, v, device(way)))
                    if final:
                        for v in views(tuple(done), axis, got, half):
                            arrived.append(Copy(book, v, sibling))
                self.steps.append(sends)
                if final:
                    self.forwards.append(arrived)
            done.append(axis)

    def run(self, step):
        if step > len(self.steps):
            return
        if step > 0:
            for copy in self.steps[step - 1]:
                copy.make().wait_recv()
        if step < len(self.steps):
            for copy in self.steps[step]:
                copy.make().start()
        if step < len(self.forwards):
            for copy in self.forwards[step]:
                copy.make().start()

    def siblings(self, first=0, last=99):
        for group in self.forwards[first:last]:
            for copy in group:
                copy.make().wait_recv()


def sizes_of(blocks, heads):
    y_lo, y_hi = 2, 2
    return heads // y_hi, y_hi, y_lo, blocks // (2 * y_lo)


def exchange_kernel(
    blocks,
    heads,
    lengths_hbm,
    positions_hbm,
    a_key,
    a_value,
    b_query,
    b_key,
    b_value,
    cache_key,
    cache_value,
    key_all,
    value_all,
    part_in,
    stat_in,
    order,
    lengths,
    positions,
    q_all,
    k_all,
    v_all,
    k_buf,
    v_buf,
    part,
    col,
    part_near,
    col_near,
    held,
    held_col,
    column,
    part_out,
    stat_out,
    send,
    recv,
    near_send,
    near_recv,
    merge_send,
    merge_recv,
    local,
):
    X, YH, YL, Z = sizes_of(blocks, heads)
    Y = YH * YL
    me, t = lax.axis_index("blk"), lax.axis_index("tensor")
    yl, z, c = me // (2 * Z), (me // 2) % Z, me % 2
    x, yh = t // YH, t % YH
    y = yh * YL + yl
    mine = yl * Z + z
    chips = YL * Z

    def dev(x, y, z, c):
        return ((y % YL) * (2 * Z) + z * 2 + c, x * YH + y // YL)

    axes = {
        "x": (X, x, lambda way: dev((x + way + X) % X, y, z, c)),
        "y": (Y, y, lambda way: dev(x, (y + way + Y) % Y, z, c)),
        "z": (Z, z, lambda way: dev(x, y, (z + way + Z) % Z, c)),
        "yl": (YL, yl, lambda way: dev(x, yh * YL + (1 - yl), z, c)),
        "yh": (YH, yh, lambda way: dev(x, (1 - yh) * YL + yl, z, c)),
    }
    sibling = dev(x, y, z, 1 - c)
    every = slice(None)
    rows = a_key.shape[0]
    cut = rows * 3 // 4
    upper, lower = pl.ds(0, cut), pl.ds(cut, rows - cut)

    def a_views(arrays, lone):
        def views(done, axis, at, half):
            chosen = arrays
            zs = every if "z" in done else (at if axis == "z" else z)
            if half is not None:
                if len(arrays) == 2:
                    chosen = arrays[half:half + 1]
                elif "z" in done:
                    zs = pl.ds(half * (Z // 2), Z // 2)
                elif half != lone:
                    chosen = []
            xs = every if "x" in done else (at if axis == "x" else x)
            if "y" in done:
                yls, yhs = every, every
            elif axis == "y":
                yls, yhs = at % YL, at // YL
            else:
                yls, yhs = yl, yh
            return [lambda a=a, r=r: a.at[yls, zs, c, xs, yhs, r] for a, r in chosen]

        return views

    def near_views(done, axis, at, half):
        chosen = [k_all, v_all] if half is None else [k_all, v_all][half:half + 1]
        return [lambda a=a: a.at[yh, at] for a in chosen]

    def far_views(done, axis, at, half):
        chosen = [k_all, v_all] if half is None else [k_all, v_all][half:half + 1]
        if axis == "yh":
            return [lambda a=a: a.at[at, x] for a in chosen]
        return [lambda a=a: a.at[1 - yh, at] for a in chosen]

    def query_views(done, axis, at, half):
        if half == 1:
            return []
        yls = every if "yl" in done else (at if axis == "yl" else yl)
        zs = at if axis == "z" else z
        return [lambda: q_all.at[yls, zs, c]]

    book = Book(send, recv)
    near = Gather(book, near_views, ["x"], axes, None)
    far = Gather(book, far_views, ["yh", "x"], axes, None)
    asked = Gather(book, query_views, ["yl", "z"], axes, sibling)
    piece_x = Gather(book, a_views([(key_all, upper)], 0), ["z*", "y", "x"], axes, sibling)
    piece_y = Gather(book, a_views([(value_all, upper)], 1), ["z*", "x", "y"], axes, sibling)
    piece_z = Gather(
        book, a_views([(key_all, lower), (value_all, lower)], 0), ["x*", "y*", "z"], axes, sibling
    )

    fresh = b_query.shape[0]
    count = k_all.shape[1] * k_all.shape[2]
    locals_ = [
        (cache_key, k_all.at[yh, x]),
        (cache_value, v_all.at[yh, x]),
        (b_query, q_all.at[yl, z, c]),
        (a_key, key_all.at[yl, z, c, x, yh]),
        (a_value, value_all.at[yl, z, c, x, yh]),
        (b_key, k_buf.at[pl.ds(count, fresh)]),
        (b_value, v_buf.at[pl.ds(count, fresh), pl.ds(0, HD)]),
        (lengths_hbm, lengths),
        (positions_hbm, positions),
    ]
    locals_ = [
        pltpu.make_async_copy(a, b, local.at[i]) for i, (a, b) in enumerate(locals_)
    ]
    for copy in locals_:
        copy.start()

    barrier = pltpu.get_barrier_semaphore()
    others = [dev((x + r) % X, y, z, c) for r in range(1, X)] + [
        dev(x, (1 - yh) * YL + yl, z, c),
        dev(x, (1 - yh) * YL + 1 - yl, z, c),
        sibling,
    ]
    for other in others:
        pl.semaphore_signal(barrier, inc=1, device_id=other, device_id_type=MESH)

    def greet(r, unused):
        pl.semaphore_signal(
            barrier, inc=1, device_id=((me + 2 * r) % blocks, t), device_id_type=MESH
        )
        return unused

    lax.fori_loop(1, chips, greet, 0)
    pl.semaphore_wait(barrier, len(others) + chips - 1)
    for copy in locals_[:-1]:
        copy.wait()

    far.run(0)
    near.run(0)
    asked.run(0)
    piece_z.run(0)
    piece_x.run(0)
    piece_y.run(0)
    column[...] = jnp.zeros(column.shape, jnp.float32)
    k_buf[count + fresh:, :] = jnp.zeros((HD - fresh, HD), jnp.bfloat16)
    v_buf[count + fresh:, :HD] = jnp.zeros((HD - fresh, HD), jnp.bfloat16)
    v_buf[count:, HD:] = jnp.ones((HD, HD), jnp.bfloat16)
    asked.run(1)
    piece_z.run(1)
    piece_x.run(1)
    piece_y.run(1)
    near.run(1)
    asked.run(2)
    piece_z.run(2)
    far.run(1)
    near.run(2)
    slots = k_all.shape[2]
    side = X * slots
    limit = lengths[me]

    def prepare(which, lead):
        row = lax.broadcasted_iota(jnp.int32, (side, HD), 0)
        live = (row // slots) * (YH * slots) + row % slots + which * slots < limit
        keys = k_all[which].reshape(side, HD).astype(jnp.float32)
        values = v_all[which].reshape(side, HD).astype(jnp.float32)
        lead = jnp.broadcast_to(lead, (side, HD))
        k_buf[:side, :] = jnp.where(live, keys, lead).astype(jnp.bfloat16)
        v_buf[:side, :HD] = jnp.where(live, values, 0.0).astype(jnp.bfloat16)
        v_buf[:side, HD:] = jnp.where(live, 1.0, 0.0).astype(jnp.bfloat16)

    prepare(yh, k_all[yh, 0][:1].astype(jnp.float32))
    asked.siblings(0, 3)

    tiles = blocks // OWNERS
    zs_tile = OWNERS // 2
    tile_rows = OWNERS * fresh
    soon = [
        (0, lambda: asked.run(3)),
        (0, lambda: piece_x.run(2)),
        (0, lambda: piece_y.run(2)),
        (1, lambda: asked.run(4)),
        (1, lambda: piece_z.run(3)),
        (2, lambda: asked.siblings(3, 5)),
        (2, lambda: far.run(2)),
        (3, lambda: asked.run(5)),
        (3, lambda: piece_x.run(3)),
        (3, lambda: piece_y.run(3)),
        (4, lambda: piece_z.run(4)),
        (6, lambda: asked.siblings(5)),
    ]
    late = [
        (0, lambda: piece_z.run(5)),
        (3, lambda: piece_z.run(6)),
        (4, lambda: piece_x.run(4)),
        (4, lambda: piece_y.run(4)),
    ]

    def serve(i, todo):
        for at in range(tiles):
            now = [act for when, act in todo if min(when, tiles - 1) == at]
            if now:
                @pl.when(i == at)
                def _():
                    for act in now:
                        act()

    def tile_of(i):
        pairs, k = Z // 2, i // 2
        away = ((k + 1) // 2) * (2 * (k % 2) - 1)
        yl_at, z_at = (yl + i) % 2, ((z // 2 + away + pairs) % pairs) * 2
        return yl_at * (2 * Z) + 2 * z_at, yl_at, z_at

    def near_copies(i):
        return [
            pltpu.make_async_remote_copy(
                src_ref=a.at[i, 1 - c],
                dst_ref=b.at[i],
                send_sem=near_send.at[n, i],
                recv_sem=near_recv.at[n, i],
                device_id=sibling,
                device_id_type=MESH,
            )
            for n, (a, b) in enumerate(((part, part_near), (col, col_near)))
        ]

    def merge_copies(source, slot, owner, sem):
        return [
            pltpu.make_async_remote_copy(
                src_ref=a,
                dst_ref=b.at[slot],
                send_sem=merge_send.at[n, sem],
                recv_sem=merge_recv.at[n, slot],
                device_id=(owner, t),
                device_id_type=MESH,
            )
            for n, (a, b) in enumerate(
                ((part_out.at[source], part_in), (stat_out.at[source // zs_tile], stat_in))
            )
        ]

    def own_copies(source):
        return [
            pltpu.make_async_copy(a, b.at[mine], local.at[n])
            for n, (a, b) in enumerate(
                ((part_out.at[source], part_in), (stat_out.at[source // zs_tile], stat_in))
            )
        ]

    lane = lax.broadcasted_iota(jnp.int32, (fresh, HD), 1)

    def finish(i):
        for copy in near_copies(i):
            copy.wait_recv()
        first, yl_at, z_at = tile_of(i)
        for n in range(zs_tile):
            ours, theirs = col[i, c, n], col_near[i, n]
            stats = []
            for h in range(2):
                base0, base1 = ours[:, h:h + 1], theirs[:, h:h + 1]
                base = jnp.maximum(base0, base1)
                share0 = ours[:, 2 + h:3 + h] * jnp.exp2(base0 - base)
                share1 = theirs[:, 2 + h:3 + h] * jnp.exp2(base1 - base)
                total = share0 + share1
                at = slice(h * HD, (h + 1) * HD)
                both = share0 * part[i, c, n, :, at].astype(jnp.float32) + share1 * part_near[
                    i, n, :, at
                ].astype(jnp.float32)
                part_out[zs_tile * i + n, :, at] = (both / total).astype(jnp.bfloat16)
                stats += [base, total]
            column[n * (HD // 2):n * (HD // 2) + fresh, :] = jnp.where(
                lane == 0,
                stats[0],
                jnp.where(lane == 1, stats[2], jnp.where(lane == 2, stats[1], stats[3])),
            )
        stat_out[i] = column[...].T[:8]
        for n in range(zs_tile):
            owner = first + 2 * n + c
            slot = yl_at * Z + z_at + n

            @pl.when(owner != me)
            def _():
                for copy in merge_copies(zs_tile * i + n, mine, owner, slot):
                    copy.start()

            @pl.when(owner == me)
            def _():
                for copy in own_copies(zs_tile * i + n):
                    copy.start()

    wide = lax.broadcasted_iota(jnp.int32, (tile_rows, HD), 1)

    def pack(bases, sums):
        return jnp.where(
            wide == 0, bases[0], jnp.where(wide == 1, bases[1], jnp.where(wide == 2, sums[0], sums[1]))
        )

    def near_step(i, unused):
        serve(i, soon)

        first, yl_at, z_at = tile_of(i)
        q = q_all[yl_at, pl.ds(z_at, zs_tile)].reshape(tile_rows, 2 * HD)
        bases, sums = [], []
        both = [dot(q[:, h * HD:(h + 1) * HD], k_buf[:side, :], NT) for h in range(2)]
        for h, scores in enumerate(both):
            base = jnp.max(scores, axis=1, keepdims=True) * SCALE2
            p = jnp.exp2(scores * SCALE2 - base).astype(jnp.bfloat16)
            acc = dot(p, v_buf[:side, :], NN)
            held[i, :, h * HD:(h + 1) * HD] = acc[:, :HD]
            bases.append(jnp.where(yh * slots < limit, base, LOWEST))
            sums.append(acc[:, HD:HD + 1])
        held_col[i] = pack(bases, sums)
        return unused

    lax.fori_loop(0, tiles, near_step, 0)
    far.run(3)
    locals_[-1].wait()

    def label(i, unused):
        order[i] = positions[i * BLOCK] // BLOCK
        return unused

    lax.fori_loop(0, order.shape[0], label, 0)
    prepare(1 - yh, k_all[0, 0][:1].astype(jnp.float32))

    def tile_step(i, unused):
        serve(i, late)

        first, yl_at, z_at = tile_of(i)
        q = q_all[yl_at, pl.ds(z_at, zs_tile)].reshape(tile_rows, 2 * HD)
        before = held_col[i]
        bases, sums, outs = [], [], []
        both = [
            (
                dot(q[:, h * HD:(h + 1) * HD], k_buf[:side, :], NT),
                dot(q[:, h * HD:(h + 1) * HD], k_buf[side:, :], NT),
            )
            for h in range(2)
        ]
        for h, (scores, extra) in enumerate(both):
            ki = lax.broadcasted_iota(jnp.int32, extra.shape, 1)
            ti = lax.broadcasted_iota(jnp.int32, extra.shape, 0) + first * fresh
            seen = jnp.logical_and(ki < fresh, ki + me * fresh <= ti)
            extra = jnp.where(seen, extra, LOWEST)
            top = jnp.maximum(
                jnp.max(scores, axis=1, keepdims=True), jnp.max(extra, axis=1, keepdims=True)
            )
            old = before[:, h:h + 1]
            base = jnp.maximum(old, top * SCALE2)
            factor = jnp.exp2(old - base)
            p = jnp.exp2(scores * SCALE2 - base).astype(jnp.bfloat16)
            p_extra = jnp.exp2(extra * SCALE2 - base).astype(jnp.bfloat16)
            acc = dot(p, v_buf[:side, :], NN) + dot(p_extra, v_buf[side:, :], NN)
            total = acc[:, HD:HD + 1] + before[:, 2 + h:3 + h] * factor
            outs.append(
                ((acc[:, :HD] + held[i, :, h * HD:(h + 1) * HD] * factor) / total).astype(
                    jnp.bfloat16
                )
            )
            bases.append(base)
            sums.append(total)
        packed = pack(bases, sums)
        for j in range(OWNERS):
            at = slice(j * fresh, (j + 1) * fresh)
            for h in range(2):
                part[i, j % 2, j // 2, :, h * HD:(h + 1) * HD] = outs[h][at]
            col[i, j % 2, j // 2] = packed[at]
        for copy in near_copies(i):
            copy.start()

        @pl.when(i > 0)
        def _():
            finish(i - 1)

        return unused

    lax.fori_loop(0, tiles, tile_step, 0)
    finish(tiles - 1)
    piece_x.run(5)
    piece_y.run(5)
    for copy in own_copies(0):
        copy.wait()

    def arrive(r, unused):
        other = (mine + r) % chips
        for copy in merge_copies(0, other, 2 * other + c, other):
            copy.wait_recv()
        return unused

    lax.fori_loop(1, chips, arrive, 0)
    for piece in (piece_x, piece_y, piece_z):
        piece.siblings()
    for copy in book.copies:
        copy.make().wait_send()

    def leave(r, unused):
        other = (mine + r) % chips
        for copy in merge_copies(0, other, 2 * other + c, other):
            copy.wait_send()
        return unused

    lax.fori_loop(1, chips, leave, 0)

    def part_ways(i, unused):
        for copy in near_copies(i):
            copy.wait_send()
        return unused

    lax.fori_loop(0, tiles, part_ways, 0)


def exchange(blocks, heads, lengths, positions, a_key, a_value, b_query, b_key, b_value, cache_key, cache_value):
    X, YH, YL, Z = sizes_of(blocks, heads)
    rows = a_key.shape[0]
    fresh = b_query.shape[0]
    slots = cache_key.shape[0]
    count = slots * X
    chips = YL * Z
    tiles = blocks // OWNERS
    half = OWNERS // 2
    whole = jax.ShapeDtypeStruct((YL, Z, 2, X, YH, rows, HD), jnp.bfloat16)
    hbm = pl.BlockSpec(memory_space=pltpu.HBM)
    anywhere = pl.BlockSpec(memory_space=pl.ANY)
    copies = 128
    return pl.pallas_call(
        functools.partial(exchange_kernel, blocks, heads),
        out_shape=(
            whole,
            whole,
            jax.ShapeDtypeStruct((chips, fresh, 2 * HD), jnp.bfloat16),
            jax.ShapeDtypeStruct((chips, 8, HD), jnp.float32),
            jax.ShapeDtypeStruct((positions.shape[0] // BLOCK,), jnp.int32),
        ),
        in_specs=[hbm] * 9,
        out_specs=[anywhere] * 4 + [pl.BlockSpec(memory_space=pltpu.SMEM)],
        scratch_shapes=[
            pltpu.SMEM(lengths.shape, jnp.int32),
            pltpu.SMEM(positions.shape, jnp.int32),
            pltpu.VMEM((YL, Z, 2, fresh, 2 * HD), jnp.bfloat16),
            pltpu.VMEM((YH, X, slots, HD), jnp.bfloat16),
            pltpu.VMEM((YH, X, slots, HD), jnp.bfloat16),
            pltpu.VMEM((count + HD, HD), jnp.bfloat16),
            pltpu.VMEM((count + HD, 2 * HD), jnp.bfloat16),
            pltpu.VMEM((tiles, 2, half, fresh, 2 * HD), jnp.bfloat16),
            pltpu.VMEM((tiles, 2, half, fresh, HD), jnp.float32),
            pltpu.VMEM((tiles, half, fresh, 2 * HD), jnp.bfloat16),
            pltpu.VMEM((tiles, half, fresh, HD), jnp.float32),
            pltpu.VMEM((tiles, OWNERS * fresh, 2 * HD), jnp.float32),
            pltpu.VMEM((tiles, OWNERS * fresh, HD), jnp.float32),
            pltpu.VMEM((HD, HD), jnp.float32),
            pltpu.VMEM((chips, fresh, 2 * HD), jnp.bfloat16),
            pltpu.VMEM((tiles, 8, HD), jnp.float32),
            pltpu.SemaphoreType.DMA((copies,)),
            pltpu.SemaphoreType.DMA((copies,)),
            pltpu.SemaphoreType.DMA((2, tiles)),
            pltpu.SemaphoreType.DMA((2, tiles)),
            pltpu.SemaphoreType.DMA((2, chips)),
            pltpu.SemaphoreType.DMA((2, chips)),
            pltpu.SemaphoreType.DMA((9,)),
        ],
        compiler_params=pltpu.CompilerParams(
            vmem_limit_bytes=32 * 2**20, collective_id=0, has_side_effects=True
        ),
        cost_estimate=pl.CostEstimate(
            flops=10_000_000_000, bytes_accessed=20_000_000, transcendentals=6_700_000
        ),
        name="exchange",
    )(
        *[
            pltpu.with_memory_space_constraint(v, pltpu.HBM)
            for v in (
                lengths, positions, a_key, a_value, b_query, b_key, b_value, cache_key, cache_value
            )
        ]
    )


def a_kernel(
    fresh, pos_ref, q_ref, key_ref, value_ref, part_ref, stat_ref, o_ref, b_ref,
    q_buf, s_buf, m_buf, acc_buf, place,
):
    total = key_ref.shape[0]
    chips = part_ref.shape[0]
    group = lax.axis_index("blk")
    own = [pos_ref[2 * group], pos_ref[2 * group + 1]]
    wholes = own[0] // CHUNK
    steps = total // CHUNK - 1
    unroll = 3 if steps % 3 == 0 else 1

    def invert(i, unused):
        place[pos_ref[i]] = i
        return unused

    lax.fori_loop(0, total, invert, 0)
    ones = jnp.ones((CHUNK * BLOCK, HD), jnp.bfloat16)
    for part in range(2):
        for h in range(2):
            q = q_ref[part * BLOCK:(part + 1) * BLOCK, h * HD:(h + 1) * HD]
            q = q.astype(jnp.float32) * SCALE2
            main = q.astype(jnp.bfloat16)
            q_buf[part, h, :, :HD] = main
            q_buf[part, h, :, HD:] = (q - main.astype(jnp.float32)).astype(jnp.bfloat16)

    def load_keys(at):
        keys = jnp.concatenate([key_ref[place[at * CHUNK + b]] for b in range(CHUNK)], axis=0)
        return jnp.concatenate([keys, keys], axis=1)

    def load_values(at):
        values = jnp.concatenate([value_ref[place[at * CHUNK + b]] for b in range(CHUNK)], axis=0)
        return jnp.concatenate([values, ones], axis=1)

    for part in range(2):
        at = own[part] // CHUNK
        keys, values = load_keys(at), load_values(at)
        for h in range(2):
            s = dot(q_buf[part, h], keys, NT)
            ki = lax.broadcasted_iota(jnp.int32, s.shape, 1) + (at * CHUNK - own[part]) * BLOCK
            qi = lax.broadcasted_iota(jnp.int32, s.shape, 0)
            s = jnp.where(ki <= qi, s, LOWEST)
            new = jnp.max(s, axis=1, keepdims=True)
            m_buf[part, h] = jnp.broadcast_to(new, (BLOCK, HD))
            p = jnp.exp2(s - new).astype(jnp.bfloat16)
            acc_buf[part, h] = dot(p, values, NN)

    def place_of(i):
        i = jnp.minimum(i, steps - 1)
        part = (i >= wholes).astype(jnp.int32)
        return part, i - part * wholes

    def score(i, h):
        part, at = place_of(i)
        return dot(q_buf[part, h], load_keys(at), NT)

    s_buf[...] = score(0, 0)

    def step(j, unused):
        ready = s_buf[...]
        for n in range(unroll):
            i = j * unroll + n
            part, at = place_of(i)
            values = load_values(at)
            for h in range(2):
                s = ready
                ready = score(i + h, 1 - h)
                old = m_buf[part, h]
                new = jnp.maximum(old, jnp.max(s, axis=1, keepdims=True))
                m_buf[part, h] = new
                factor = jnp.exp2(old - new)
                p = jnp.exp2(s - new[:, :1]).astype(jnp.bfloat16)
                acc_buf[part, h] = acc_buf[part, h] * factor[:, :1] + dot(p, values, NN)
        s_buf[...] = ready
        return unused

    lax.fori_loop(0, steps // unroll, step, 0)
    for part in range(2):
        for h in range(2):
            acc = acc_buf[part, h]
            o_ref[part * BLOCK:(part + 1) * BLOCK, h * HD:(h + 1) * HD] = (
                acc[:, :HD] / acc[:, HD:]
            ).astype(jnp.bfloat16)

    odd = (group // 2) % 2 == 1
    for h in range(2):
        base = stat_ref[:, h, :]
        best = jnp.max(base, axis=0, keepdims=True)
        share = stat_ref[:, 2 + h, :] * jnp.exp2(base - best)
        share = jnp.concatenate(
            [share, jnp.zeros((HD - chips, HD), jnp.float32)], axis=0
        ).T
        share = jnp.where(odd, share[HD // 2:HD // 2 + fresh], share[:fresh])
        numer = jnp.zeros((fresh, HD), jnp.float32)
        for g in range(chips):
            numer = numer + share[:, g:g + 1] * part_ref[g, :, h * HD:(h + 1) * HD].astype(
                jnp.float32
            )
        denom = jnp.sum(share, axis=1, keepdims=True)
        b_ref[:, h * HD:(h + 1) * HD] = (numer / denom).astype(jnp.bfloat16)


def attend_a(fresh, positions, queries, keys, values, part, stat):
    total = positions.shape[0]
    vmem = pl.BlockSpec(memory_space=pltpu.VMEM)
    return pl.pallas_call(
        functools.partial(a_kernel, fresh),
        out_shape=(
            jax.ShapeDtypeStruct(queries.shape, jnp.bfloat16),
            jax.ShapeDtypeStruct((fresh, 2 * HD), jnp.bfloat16),
        ),
        in_specs=[pl.BlockSpec(memory_space=pltpu.SMEM)] + [vmem] * 5,
        out_specs=[vmem, vmem],
        scratch_shapes=[
            pltpu.VMEM((2, 2, BLOCK, 2 * HD), jnp.bfloat16),
            pltpu.VMEM((BLOCK, CHUNK * BLOCK), jnp.float32),
            pltpu.VMEM((2, 2, BLOCK, HD), jnp.float32),
            pltpu.VMEM((2, 2, BLOCK, 2 * HD), jnp.float32),
            pltpu.SMEM((total,), jnp.int32),
        ],
        compiler_params=pltpu.CompilerParams(vmem_limit_bytes=32 * 2**20),
        cost_estimate=pl.CostEstimate(
            flops=10_000_000_000, bytes_accessed=9_000_000, transcendentals=8_500_000
        ),
        name="attend_a",
    )(positions, queries, keys.reshape(total, -1, HD), values.reshape(total, -1, HD), part, stat)


def shards(
    blocks,
    heads,
    a_query,
    a_key,
    a_value,
    b_query,
    b_key,
    b_value,
    cache_key,
    cache_value,
    a_positions,
    cache_lengths,
):
    *gathered, order = exchange(
        blocks,
        heads,
        cache_lengths,
        a_positions,
        a_key,
        a_value,
        b_query,
        b_key,
        b_value,
        cache_key,
        cache_value,
    )
    return attend_a(b_query.shape[0], order, a_query, *gathered)


def solution(mesh):
    in_specs = (
        P("blk", "tensor"),
        P(("blk", "tensor"), None),
        P(("blk", "tensor"), None),
        P("blk", "tensor"),
        P("blk", None),
        P("blk", None),
        P(("blk", "tensor"), None),
        P(("blk", "tensor"), None),
        P(),
        P(),
    )
    out_specs = (P("blk", "tensor"), P("blk", "tensor"))
    body = functools.partial(shards, mesh.shape["blk"], mesh.shape["tensor"])
    return jax.shard_map(body, mesh=mesh, in_specs=in_specs, out_specs=out_specs, check_vma=False)
```

```python
import functools
import math

import jax
import jax.numpy as jnp
from jax import lax
from jax.experimental import pallas as pl
from jax.experimental.pallas import tpu as pltpu
from jax.sharding import PartitionSpec as P

HD = 128
BLOCK = 256
CHUNK = 4
OWNERS = 4
SCALE2 = HD ** (-0.5) * math.log2(math.e)
LOWEST = -1e30
NT = (((1,), (1,)), ((), ()))
NN = (((1,), (0,)), ((), ()))
MESH = pl.DeviceIdType.MESH


def dot(a, b, dims):
    return lax.dot_general(a, b, dims, preferred_element_type=jnp.float32)


class Copy:
    def __init__(self, book, view, device):
        self.book, self.view, self.device = book, view, device
        self.index = len(book.copies)
        book.copies.append(self)

    def make(self):
        return pltpu.make_async_remote_copy(
            src_ref=self.view(),
            dst_ref=self.view(),
            send_sem=self.book.send.at[self.index],
            recv_sem=self.book.recv.at[self.index],
            device_id=self.device,
            device_id_type=MESH,
        )


class Book:
    def __init__(self, send, recv):
        self.send, self.recv, self.copies = send, recv, []


class Gather:
    def __init__(self, book, views, order, axes, sibling):
        self.steps, self.forwards = [], []
        done = []
        for number, name in enumerate(order):
            axis = name.rstrip("*")
            size, at, device = axes[axis]
            final = number == len(order) - 1 and sibling is not None
            if final:
                self.forwards = [[] for step in self.steps]
                self.forwards.append(
                    [Copy(book, v, sibling) for v in views(tuple(done), axis, at, None)]
                )
            if name.endswith("*"):
                sends = []
                for way in range(1, size):
                    for v in views(tuple(done), axis, at, None):
                        sends.append(Copy(book, v, device(way)))
                if sends:
                    self.steps.append(sends)
                done.append(axis)
                continue
            for k in range(1, size // 2 + 1):
                sends, arrived = [], []
                for way in (1, -1):
                    if size == 2 and way == -1:
                        continue
                    half = None
                    if 2 * k == size and size > 2:
                        half = 0 if way == 1 else 1
                    out = (at - way * (k - 1) + 2 * size) % size
                    got = (at - way * k + 2 * size) % size
                    for v in views(tuple(done), axis, out, half):
                        sends.append(Copy(book, v, device(way)))
                    if final:
                        for v in views(tuple(done), axis, got, half):
                            arrived.append(Copy(book, v, sibling))
                self.steps.append(sends)
                if final:
                    self.forwards.append(arrived)
            done.append(axis)

    def run(self, step):
        if step > len(self.steps):
            return
        if step > 0:
            for copy in self.steps[step - 1]:
                copy.make().wait_recv()
        if step < len(self.steps):
            for copy in self.steps[step]:
                copy.make().start()
        if step < len(self.forwards):
            for copy in self.forwards[step]:
                copy.make().start()

    def siblings(self, first=0, last=99):
        for group in self.forwards[first:last]:
            for copy in group:
                copy.make().wait_recv()


def sizes_of(blocks, heads):
    y_lo, y_hi = 2, 2
    return heads // y_hi, y_hi, y_lo, blocks // (2 * y_lo)


def exchange_kernel(
    blocks,
    heads,
    lengths_hbm,
    positions_hbm,
    a_key,
    a_value,
    b_query,
    b_key,
    b_value,
    cache_key,
    cache_value,
    key_all,
    value_all,
    part_in,
    stat_in,
    order,
    lengths,
    positions,
    q_all,
    k_all,
    v_all,
    k_buf,
    v_buf,
    part,
    col,
    part_near,
    col_near,
    held,
    held_col,
    column,
    part_out,
    stat_out,
    send,
    recv,
    near_send,
    near_recv,
    merge_send,
    merge_recv,
    local,
):
    X, YH, YL, Z = sizes_of(blocks, heads)
    Y = YH * YL
    me, t = lax.axis_index("blk"), lax.axis_index("tensor")
    yl, z, c = me // (2 * Z), (me // 2) % Z, me % 2
    x, yh = t // YH, t % YH
    y = yh * YL + yl
    mine = yl * Z + z
    chips = YL * Z

    def dev(x, y, z, c):
        return ((y % YL) * (2 * Z) + z * 2 + c, x * YH + y // YL)

    axes = {
        "x": (X, x, lambda way: dev((x + way + X) % X, y, z, c)),
        "y": (Y, y, lambda way: dev(x, (y + way + Y) % Y, z, c)),
        "z": (Z, z, lambda way: dev(x, y, (z + way + Z) % Z, c)),
        "yl": (YL, yl, lambda way: dev(x, yh * YL + (1 - yl), z, c)),
        "yh": (YH, yh, lambda way: dev(x, (1 - yh) * YL + yl, z, c)),
    }
    sibling = dev(x, y, z, 1 - c)
    every = slice(None)
    rows = a_key.shape[0]
    cut = rows * 3 // 4
    upper, lower = pl.ds(0, cut), pl.ds(cut, rows - cut)

    def a_views(arrays, lone):
        def views(done, axis, at, half):
            chosen = arrays
            zs = every if "z" in done else (at if axis == "z" else z)
            if half is not None:
                if len(arrays) == 2:
                    chosen = arrays[half:half + 1]
                elif "z" in done:
                    zs = pl.ds(half * (Z // 2), Z // 2)
                elif half != lone:
                    chosen = []
            xs = every if "x" in done else (at if axis == "x" else x)
            if "y" in done:
                yls, yhs = every, every
            elif axis == "y":
                yls, yhs = at % YL, at // YL
            else:
                yls, yhs = yl, yh
            return [lambda a=a, r=r: a.at[yls, zs, c, xs, yhs, r] for a, r in chosen]

        return views

    def near_views(done, axis, at, half):
        chosen = [k_all, v_all] if half is None else [k_all, v_all][half:half + 1]
        return [lambda a=a: a.at[yh, at] for a in chosen]

    def far_views(done, axis, at, half):
        chosen = [k_all, v_all] if half is None else [k_all, v_all][half:half + 1]
        if axis == "yh":
            return [lambda a=a: a.at[at, x] for a in chosen]
        return [lambda a=a: a.at[1 - yh, at] for a in chosen]

    def query_views(done, axis, at, half):
        if half == 1:
            return []
        yls = every if "yl" in done else (at if axis == "yl" else yl)
        zs = at if axis == "z" else z
        return [lambda: q_all.at[yls, zs, c]]

    book = Book(send, recv)
    near = Gather(book, near_views, ["x"], axes, None)
    far = Gather(book, far_views, ["yh", "x"], axes, None)
    asked = Gather(book, query_views, ["yl", "z"], axes, sibling)
    piece_x = Gather(book, a_views([(key_all, upper)], 0), ["z*", "y*", "x"], axes, sibling)
    piece_y = Gather(book, a_views([(value_all, upper)], 1), ["z*", "x*", "y"], axes, sibling)
    piece_z = Gather(
        book, a_views([(key_all, lower), (value_all, lower)], 0), ["x*", "y*", "z"], axes, sibling
    )

    fresh = b_query.shape[0]
    count = k_all.shape[1] * k_all.shape[2]
    locals_ = [
        (cache_key, k_all.at[yh, x]),
        (cache_value, v_all.at[yh, x]),
        (b_query, q_all.at[yl, z, c]),
        (a_key, key_all.at[yl, z, c, x, yh]),
        (a_value, value_all.at[yl, z, c, x, yh]),
        (b_key, k_buf.at[pl.ds(count, fresh)]),
        (b_value, v_buf.at[pl.ds(count, fresh), pl.ds(0, HD)]),
        (lengths_hbm, lengths),
        (positions_hbm, positions),
    ]
    locals_ = [
        pltpu.make_async_copy(a, b, local.at[i]) for i, (a, b) in enumerate(locals_)
    ]
    for copy in locals_:
        copy.start()

    barrier = pltpu.get_barrier_semaphore()
    others = [dev((x + r) % X, y, z, c) for r in range(1, X)] + [
        dev(x, (1 - yh) * YL + yl, z, c),
        dev(x, (1 - yh) * YL + 1 - yl, z, c),
        sibling,
    ]
    for other in others:
        pl.semaphore_signal(barrier, inc=1, device_id=other, device_id_type=MESH)

    def greet(r, unused):
        pl.semaphore_signal(
            barrier, inc=1, device_id=((me + 2 * r) % blocks, t), device_id_type=MESH
        )
        return unused

    lax.fori_loop(1, chips, greet, 0)
    pl.semaphore_wait(barrier, len(others) + chips - 1)
    for copy in locals_[:-1]:
        copy.wait()

    asked.run(0)
    piece_x.run(0)
    piece_y.run(0)
    near.run(0)
    piece_z.run(0)
    far.run(0)
    column[...] = jnp.zeros(column.shape, jnp.float32)
    k_buf[count + fresh:, :] = jnp.zeros((HD - fresh, HD), jnp.bfloat16)
    v_buf[count + fresh:, :HD] = jnp.zeros((HD - fresh, HD), jnp.bfloat16)
    v_buf[count:, HD:] = jnp.ones((HD, HD), jnp.bfloat16)
    asked.run(1)
    piece_x.run(1)
    piece_y.run(1)
    piece_z.run(1)
    near.run(1)
    asked.run(2)
    piece_z.run(2)
    far.run(1)
    piece_x.run(2)
    piece_y.run(2)
    near.run(2)
    slots = k_all.shape[2]
    side = X * slots
    limit = lengths[me]

    def prepare(which, lead):
        row = lax.broadcasted_iota(jnp.int32, (side, HD), 0)
        live = (row // slots) * (YH * slots) + row % slots + which * slots < limit
        keys = k_all[which].reshape(side, HD).astype(jnp.float32)
        values = v_all[which].reshape(side, HD).astype(jnp.float32)
        lead = jnp.broadcast_to(lead, (side, HD))
        k_buf[:side, :] = jnp.where(live, keys, lead).astype(jnp.bfloat16)
        v_buf[:side, :HD] = jnp.where(live, values, 0.0).astype(jnp.bfloat16)
        v_buf[:side, HD:] = jnp.where(live, 1.0, 0.0).astype(jnp.bfloat16)

    prepare(yh, k_all[yh, 0][:1].astype(jnp.float32))
    asked.siblings(0, 3)

    tiles = blocks // OWNERS
    zs_tile = OWNERS // 2
    tile_rows = OWNERS * fresh
    soon = [
        (0, lambda: asked.run(3)),
        (1, lambda: asked.run(4)),
        (1, lambda: piece_z.run(3)),
        (2, lambda: asked.siblings(3, 5)),
        (2, lambda: far.run(2)),
        (3, lambda: asked.run(5)),
        (4, lambda: piece_z.run(4)),
        (6, lambda: asked.siblings(5)),
    ]
    late = [
        (0, lambda: piece_x.run(3)),
        (0, lambda: piece_y.run(3)),
        (0, lambda: piece_z.run(5)),
        (3, lambda: piece_z.run(6)),
        (6, lambda: piece_x.run(4)),
        (6, lambda: piece_y.run(4)),
    ]

    def serve(i, todo):
        for at in range(tiles):
            now = [act for when, act in todo if min(when, tiles - 1) == at]
            if now:
                @pl.when(i == at)
                def _():
                    for act in now:
                        act()

    def tile_of(i):
        pairs, k = Z // 2, i // 2
        away = ((k + 1) // 2) * (2 * (k % 2) - 1)
        yl_at, z_at = (yl + i) % 2, ((z // 2 + away + pairs) % pairs) * 2
        return yl_at * (2 * Z) + 2 * z_at, yl_at, z_at

    def near_copies(i):
        return [
            pltpu.make_async_remote_copy(
                src_ref=a.at[i, 1 - c],
                dst_ref=b.at[i],
                send_sem=near_send.at[n, i],
                recv_sem=near_recv.at[n, i],
                device_id=sibling,
                device_id_type=MESH,
            )
            for n, (a, b) in enumerate(((part, part_near), (col, col_near)))
        ]

    def merge_copies(source, slot, owner, sem):
        return [
            pltpu.make_async_remote_copy(
                src_ref=a,
                dst_ref=b.at[slot],
                send_sem=merge_send.at[n, sem],
                recv_sem=merge_recv.at[n, slot],
                device_id=(owner, t),
                device_id_type=MESH,
            )
            for n, (a, b) in enumerate(
                ((part_out.at[source], part_in), (stat_out.at[source // zs_tile], stat_in))
            )
        ]

    def own_copies(source):
        return [
            pltpu.make_async_copy(a, b.at[mine], local.at[n])
            for n, (a, b) in enumerate(
                ((part_out.at[source], part_in), (stat_out.at[source // zs_tile], stat_in))
            )
        ]

    lane = lax.broadcasted_iota(jnp.int32, (fresh, HD), 1)

    def finish(i):
        for copy in near_copies(i):
            copy.wait_recv()
        first, yl_at, z_at = tile_of(i)
        for n in range(zs_tile):
            ours, theirs = col[i, c, n], col_near[i, n]
            stats = []
            for h in range(2):
                base0, base1 = ours[:, h:h + 1], theirs[:, h:h + 1]
                base = jnp.maximum(base0, base1)
                share0 = ours[:, 2 + h:3 + h] * jnp.exp2(base0 - base)
                share1 = theirs[:, 2 + h:3 + h] * jnp.exp2(base1 - base)
                total = share0 + share1
                at = slice(h * HD, (h + 1) * HD)
                both = share0 * part[i, c, n, :, at].astype(jnp.float32) + share1 * part_near[
                    i, n, :, at
                ].astype(jnp.float32)
                part_out[zs_tile * i + n, :, at] = (both / total).astype(jnp.bfloat16)
                stats += [base, total]
            column[n * (HD // 2):n * (HD // 2) + fresh, :] = jnp.where(
                lane == 0,
                stats[0],
                jnp.where(lane == 1, stats[2], jnp.where(lane == 2, stats[1], stats[3])),
            )
        stat_out[i] = column[...].T[:8]
        for n in range(zs_tile):
            owner = first + 2 * n + c
            slot = yl_at * Z + z_at + n

            @pl.when(owner != me)
            def _():
                for copy in merge_copies(zs_tile * i + n, mine, owner, slot):
                    copy.start()

            @pl.when(owner == me)
            def _():
                for copy in own_copies(zs_tile * i + n):
                    copy.start()

    wide = lax.broadcasted_iota(jnp.int32, (tile_rows, HD), 1)

    def pack(bases, sums):
        return jnp.where(
            wide == 0, bases[0], jnp.where(wide == 1, bases[1], jnp.where(wide == 2, sums[0], sums[1]))
        )

    def near_step(i, unused):
        serve(i, soon)

        first, yl_at, z_at = tile_of(i)
        q = q_all[yl_at, pl.ds(z_at, zs_tile)].reshape(tile_rows, 2 * HD)
        bases, sums = [], []
        both = [dot(q[:, h * HD:(h + 1) * HD], k_buf[:side, :], NT) for h in range(2)]
        for h, scores in enumerate(both):
            base = jnp.max(scores, axis=1, keepdims=True) * SCALE2
            p = jnp.exp2(scores * SCALE2 - base).astype(jnp.bfloat16)
            acc = dot(p, v_buf[:side, :], NN)
            held[i, :, h * HD:(h + 1) * HD] = acc[:, :HD]
            bases.append(jnp.where(yh * slots < limit, base, LOWEST))
            sums.append(acc[:, HD:HD + 1])
        held_col[i] = pack(bases, sums)
        return unused

    lax.fori_loop(0, tiles, near_step, 0)
    far.run(3)
    locals_[-1].wait()

    def label(i, unused):
        order[i] = positions[i * BLOCK] // BLOCK
        return unused

    lax.fori_loop(0, order.shape[0], label, 0)
    prepare(1 - yh, k_all[0, 0][:1].astype(jnp.float32))

    def tile_step(i, unused):
        serve(i, late)

        first, yl_at, z_at = tile_of(i)
        q = q_all[yl_at, pl.ds(z_at, zs_tile)].reshape(tile_rows, 2 * HD)
        before = held_col[i]
        bases, sums, outs = [], [], []
        both = [
            (
                dot(q[:, h * HD:(h + 1) * HD], k_buf[:side, :], NT),
                dot(q[:, h * HD:(h + 1) * HD], k_buf[side:, :], NT),
            )
            for h in range(2)
        ]
        for h, (scores, extra) in enumerate(both):
            ki = lax.broadcasted_iota(jnp.int32, extra.shape, 1)
            ti = lax.broadcasted_iota(jnp.int32, extra.shape, 0) + first * fresh
            seen = jnp.logical_and(ki < fresh, ki + me * fresh <= ti)
            extra = jnp.where(seen, extra, LOWEST)
            top = jnp.maximum(
                jnp.max(scores, axis=1, keepdims=True), jnp.max(extra, axis=1, keepdims=True)
            )
            old = before[:, h:h + 1]
            base = jnp.maximum(old, top * SCALE2)
            factor = jnp.exp2(old - base)
            p = jnp.exp2(scores * SCALE2 - base).astype(jnp.bfloat16)
            p_extra = jnp.exp2(extra * SCALE2 - base).astype(jnp.bfloat16)
            acc = dot(p, v_buf[:side, :], NN) + dot(p_extra, v_buf[side:, :], NN)
            total = acc[:, HD:HD + 1] + before[:, 2 + h:3 + h] * factor
            outs.append(
                ((acc[:, :HD] + held[i, :, h * HD:(h + 1) * HD] * factor) / total).astype(
                    jnp.bfloat16
                )
            )
            bases.append(base)
            sums.append(total)
        packed = pack(bases, sums)
        for j in range(OWNERS):
            at = slice(j * fresh, (j + 1) * fresh)
            for h in range(2):
                part[i, j % 2, j // 2, :, h * HD:(h + 1) * HD] = outs[h][at]
            col[i, j % 2, j // 2] = packed[at]
        for copy in near_copies(i):
            copy.start()

        @pl.when(i > 0)
        def _():
            finish(i - 1)

        return unused

    lax.fori_loop(0, tiles, tile_step, 0)
    finish(tiles - 1)
    for copy in own_copies(0):
        copy.wait()

    def arrive(r, unused):
        other = (mine + r) % chips
        for copy in merge_copies(0, other, 2 * other + c, other):
            copy.wait_recv()
        return unused

    lax.fori_loop(1, chips, arrive, 0)
    for piece in (piece_x, piece_y, piece_z):
        piece.siblings()
    for copy in book.copies:
        copy.make().wait_send()

    def leave(r, unused):
        other = (mine + r) % chips
        for copy in merge_copies(0, other, 2 * other + c, other):
            copy.wait_send()
        return unused

    lax.fori_loop(1, chips, leave, 0)

    def part_ways(i, unused):
        for copy in near_copies(i):
            copy.wait_send()
        return unused

    lax.fori_loop(0, tiles, part_ways, 0)


def exchange(blocks, heads, lengths, positions, a_key, a_value, b_query, b_key, b_value, cache_key, cache_value):
    X, YH, YL, Z = sizes_of(blocks, heads)
    rows = a_key.shape[0]
    fresh = b_query.shape[0]
    slots = cache_key.shape[0]
    count = slots * X
    chips = YL * Z
    tiles = blocks // OWNERS
    half = OWNERS // 2
    whole = jax.ShapeDtypeStruct((YL, Z, 2, X, YH, rows, HD), jnp.bfloat16)
    hbm = pl.BlockSpec(memory_space=pltpu.HBM)
    anywhere = pl.BlockSpec(memory_space=pl.ANY)
    copies = 128
    return pl.pallas_call(
        functools.partial(exchange_kernel, blocks, heads),
        out_shape=(
            whole,
            whole,
            jax.ShapeDtypeStruct((chips, fresh, 2 * HD), jnp.bfloat16),
            jax.ShapeDtypeStruct((chips, 8, HD), jnp.float32),
            jax.ShapeDtypeStruct((positions.shape[0] // BLOCK,), jnp.int32),
        ),
        in_specs=[hbm] * 9,
        out_specs=[anywhere] * 4 + [pl.BlockSpec(memory_space=pltpu.SMEM)],
        scratch_shapes=[
            pltpu.SMEM(lengths.shape, jnp.int32),
            pltpu.SMEM(positions.shape, jnp.int32),
            pltpu.VMEM((YL, Z, 2, fresh, 2 * HD), jnp.bfloat16),
            pltpu.VMEM((YH, X, slots, HD), jnp.bfloat16),
            pltpu.VMEM((YH, X, slots, HD), jnp.bfloat16),
            pltpu.VMEM((count + HD, HD), jnp.bfloat16),
            pltpu.VMEM((count + HD, 2 * HD), jnp.bfloat16),
            pltpu.VMEM((tiles, 2, half, fresh, 2 * HD), jnp.bfloat16),
            pltpu.VMEM((tiles, 2, half, fresh, HD), jnp.float32),
            pltpu.VMEM((tiles, half, fresh, 2 * HD), jnp.bfloat16),
            pltpu.VMEM((tiles, half, fresh, HD), jnp.float32),
            pltpu.VMEM((tiles, OWNERS * fresh, 2 * HD), jnp.float32),
            pltpu.VMEM((tiles, OWNERS * fresh, HD), jnp.float32),
            pltpu.VMEM((HD, HD), jnp.float32),
            pltpu.VMEM((chips, fresh, 2 * HD), jnp.bfloat16),
            pltpu.VMEM((tiles, 8, HD), jnp.float32),
            pltpu.SemaphoreType.DMA((copies,)),
            pltpu.SemaphoreType.DMA((copies,)),
            pltpu.SemaphoreType.DMA((2, tiles)),
            pltpu.SemaphoreType.DMA((2, tiles)),
            pltpu.SemaphoreType.DMA((2, chips)),
            pltpu.SemaphoreType.DMA((2, chips)),
            pltpu.SemaphoreType.DMA((9,)),
        ],
        compiler_params=pltpu.CompilerParams(
            vmem_limit_bytes=32 * 2**20, collective_id=0, has_side_effects=True
        ),
        cost_estimate=pl.CostEstimate(
            flops=10_000_000_000, bytes_accessed=20_000_000, transcendentals=6_700_000
        ),
        name="exchange",
    )(
        *[
            pltpu.with_memory_space_constraint(v, pltpu.HBM)
            for v in (
                lengths, positions, a_key, a_value, b_query, b_key, b_value, cache_key, cache_value
            )
        ]
    )


def a_kernel(
    fresh, pos_ref, q_ref, key_ref, value_ref, part_ref, stat_ref, o_ref, b_ref,
    q_buf, s_buf, m_buf, acc_buf, place,
):
    total = key_ref.shape[0]
    chips = part_ref.shape[0]
    group = lax.axis_index("blk")
    own = [pos_ref[2 * group], pos_ref[2 * group + 1]]
    wholes = own[0] // CHUNK
    steps = total // CHUNK - 1
    unroll = 5 if steps % 5 == 0 else 1

    def invert(i, unused):
        place[pos_ref[i]] = i
        return unused

    lax.fori_loop(0, total, invert, 0)
    ones = jnp.ones((CHUNK * BLOCK, HD), jnp.bfloat16)
    for part in range(2):
        for h in range(2):
            q = q_ref[part * BLOCK:(part + 1) * BLOCK, h * HD:(h + 1) * HD]
            q = q.astype(jnp.float32) * SCALE2
            main = q.astype(jnp.bfloat16)
            q_buf[part, h, :, :HD] = main
            q_buf[part, h, :, HD:] = (q - main.astype(jnp.float32)).astype(jnp.bfloat16)

    def load_keys(at):
        keys = jnp.concatenate([key_ref[place[at * CHUNK + b]] for b in range(CHUNK)], axis=0)
        return jnp.concatenate([keys, keys], axis=1)

    def load_values(at):
        values = jnp.concatenate([value_ref[place[at * CHUNK + b]] for b in range(CHUNK)], axis=0)
        return jnp.concatenate([values, ones], axis=1)

    for part in range(2):
        at = own[part] // CHUNK
        keys, values = load_keys(at), load_values(at)
        for h in range(2):
            s = dot(q_buf[part, h], keys, NT)
            ki = lax.broadcasted_iota(jnp.int32, s.shape, 1) + (at * CHUNK - own[part]) * BLOCK
            qi = lax.broadcasted_iota(jnp.int32, s.shape, 0)
            s = jnp.where(ki <= qi, s, LOWEST)
            new = jnp.max(s, axis=1, keepdims=True)
            m_buf[part, h] = jnp.broadcast_to(new, (BLOCK, HD))
            p = jnp.exp2(s - new).astype(jnp.bfloat16)
            acc_buf[part, h] = dot(p, values, NN)

    def place_of(i):
        i = jnp.minimum(i, steps - 1)
        part = (i >= wholes).astype(jnp.int32)
        return part, i - part * wholes

    def score(i, h):
        part, at = place_of(i)
        return dot(q_buf[part, h], load_keys(at), NT)

    s_buf[...] = score(0, 0)

    def step(j, unused):
        ready = s_buf[...]
        for n in range(unroll):
            i = j * unroll + n
            part, at = place_of(i)
            values = load_values(at)
            for h in range(2):
                s = ready
                ready = score(i + h, 1 - h)
                old = m_buf[part, h]
                new = jnp.maximum(old, jnp.max(s, axis=1, keepdims=True))
                m_buf[part, h] = new
                factor = jnp.exp2(old - new)
                p = jnp.exp2(s - new[:, :1]).astype(jnp.bfloat16)
                acc_buf[part, h] = acc_buf[part, h] * factor[:, :1] + dot(p, values, NN)
        s_buf[...] = ready
        return unused

    lax.fori_loop(0, steps // unroll, step, 0)
    for part in range(2):
        for h in range(2):
            acc = acc_buf[part, h]
            o_ref[part * BLOCK:(part + 1) * BLOCK, h * HD:(h + 1) * HD] = (
                acc[:, :HD] / acc[:, HD:]
            ).astype(jnp.bfloat16)

    odd = (group // 2) % 2 == 1
    for h in range(2):
        base = stat_ref[:, h, :]
        best = jnp.max(base, axis=0, keepdims=True)
        share = stat_ref[:, 2 + h, :] * jnp.exp2(base - best)
        share = jnp.concatenate(
            [share, jnp.zeros((HD - chips, HD), jnp.float32)], axis=0
        ).T
        share = jnp.where(odd, share[HD // 2:HD // 2 + fresh], share[:fresh])
        numer = jnp.zeros((fresh, HD), jnp.float32)
        for g in range(chips):
            numer = numer + share[:, g:g + 1] * part_ref[g, :, h * HD:(h + 1) * HD].astype(
                jnp.float32
            )
        denom = jnp.sum(share, axis=1, keepdims=True)
        b_ref[:, h * HD:(h + 1) * HD] = (numer / denom).astype(jnp.bfloat16)


def attend_a(fresh, positions, queries, keys, values, part, stat):
    total = positions.shape[0]
    vmem = pl.BlockSpec(memory_space=pltpu.VMEM)
    return pl.pallas_call(
        functools.partial(a_kernel, fresh),
        out_shape=(
            jax.ShapeDtypeStruct(queries.shape, jnp.bfloat16),
            jax.ShapeDtypeStruct((fresh, 2 * HD), jnp.bfloat16),
        ),
        in_specs=[pl.BlockSpec(memory_space=pltpu.SMEM)] + [vmem] * 5,
        out_specs=[vmem, vmem],
        scratch_shapes=[
            pltpu.VMEM((2, 2, BLOCK, 2 * HD), jnp.bfloat16),
            pltpu.VMEM((BLOCK, CHUNK * BLOCK), jnp.float32),
            pltpu.VMEM((2, 2, BLOCK, HD), jnp.float32),
            pltpu.VMEM((2, 2, BLOCK, 2 * HD), jnp.float32),
            pltpu.SMEM((total,), jnp.int32),
        ],
        compiler_params=pltpu.CompilerParams(vmem_limit_bytes=32 * 2**20),
        cost_estimate=pl.CostEstimate(
            flops=10_000_000_000, bytes_accessed=9_000_000, transcendentals=8_500_000
        ),
        name="attend_a",
    )(positions, queries, keys.reshape(total, -1, HD), values.reshape(total, -1, HD), part, stat)


def shards(
    blocks,
    heads,
    a_query,
    a_key,
    a_value,
    b_query,
    b_key,
    b_value,
    cache_key,
    cache_value,
    a_positions,
    cache_lengths,
):
    *gathered, order = exchange(
        blocks,
        heads,
        cache_lengths,
        a_positions,
        a_key,
        a_value,
        b_query,
        b_key,
        b_value,
        cache_key,
        cache_value,
    )
    return attend_a(b_query.shape[0], order, a_query, *gathered)


def solution(mesh):
    in_specs = (
        P("blk", "tensor"),
        P(("blk", "tensor"), None),
        P(("blk", "tensor"), None),
        P("blk", "tensor"),
        P("blk", None),
        P("blk", None),
        P(("blk", "tensor"), None),
        P(("blk", "tensor"), None),
        P(),
        P(),
    )
    out_specs = (P("blk", "tensor"), P("blk", "tensor"))
    body = functools.partial(shards, mesh.shape["blk"], mesh.shape["tensor"])
    return jax.shard_map(body, mesh=mesh, in_specs=in_specs, out_specs=out_specs, check_vma=False)
```

```python
import functools
import math

import jax
import jax.numpy as jnp
from jax import lax
from jax.experimental import pallas as pl
from jax.experimental.pallas import tpu as pltpu
from jax.sharding import PartitionSpec as P

HD = 128
BLOCK = 256
CHUNK = 4
OWNERS = 8
SCALE2 = HD ** (-0.5) * math.log2(math.e)
LOWEST = -1e30
NT = (((1,), (1,)), ((), ()))
NN = (((1,), (0,)), ((), ()))
MESH = pl.DeviceIdType.MESH


def dot(a, b, dims):
    return lax.dot_general(a, b, dims, preferred_element_type=jnp.float32)


class Copy:
    def __init__(self, book, view, device):
        self.book, self.view, self.device = book, view, device
        self.index = len(book.copies)
        book.copies.append(self)

    def make(self):
        return pltpu.make_async_remote_copy(
            src_ref=self.view(),
            dst_ref=self.view(),
            send_sem=self.book.send.at[self.index],
            recv_sem=self.book.recv.at[self.index],
            device_id=self.device,
            device_id_type=MESH,
        )


class Book:
    def __init__(self, send, recv):
        self.send, self.recv, self.copies = send, recv, []


class Gather:
    def __init__(self, book, views, order, axes, sibling):
        self.steps, self.forwards = [], []
        done = []
        for number, name in enumerate(order):
            axis = name.rstrip("*")
            size, at, device = axes[axis]
            final = number == len(order) - 1 and sibling is not None
            if final:
                self.forwards = [[] for step in self.steps]
                self.forwards.append(
                    [Copy(book, v, sibling) for v in views(tuple(done), axis, at, None)]
                )
            if name.endswith("*"):
                sends = []
                for way in range(1, size):
                    for v in views(tuple(done), axis, at, None):
                        sends.append(Copy(book, v, device(way)))
                if sends:
                    self.steps.append(sends)
                done.append(axis)
                continue
            for k in range(1, size // 2 + 1):
                sends, arrived = [], []
                for way in (1, -1):
                    if size == 2 and way == -1:
                        continue
                    half = None
                    if 2 * k == size and size > 2:
                        half = 0 if way == 1 else 1
                    out = (at - way * (k - 1) + 2 * size) % size
                    got = (at - way * k + 2 * size) % size
                    for v in views(tuple(done), axis, out, half):
                        sends.append(Copy(book, v, device(way)))
                    if final:
                        for v in views(tuple(done), axis, got, half):
                            arrived.append(Copy(book, v, sibling))
                self.steps.append(sends)
                if final:
                    self.forwards.append(arrived)
            done.append(axis)

    def run(self, step):
        if step > len(self.steps):
            return
        if step > 0:
            for copy in self.steps[step - 1]:
                copy.make().wait_recv()
        if step < len(self.steps):
            for copy in self.steps[step]:
                copy.make().start()
        if step < len(self.forwards):
            for copy in self.forwards[step]:
                copy.make().start()

    def siblings(self, first=0, last=99):
        for group in self.forwards[first:last]:
            for copy in group:
                copy.make().wait_recv()


def sizes_of(blocks, heads):
    y_lo, y_hi = 2, 2
    return heads // y_hi, y_hi, y_lo, blocks // (2 * y_lo)


def exchange_kernel(
    blocks,
    heads,
    lengths_hbm,
    positions_hbm,
    a_key,
    a_value,
    b_query,
    b_key,
    b_value,
    cache_key,
    cache_value,
    key_all,
    value_all,
    part_in,
    stat_in,
    order,
    lengths,
    positions,
    q_all,
    k_all,
    v_all,
    k_buf,
    v_buf,
    part,
    col,
    part_near,
    col_near,
    held,
    held_col,
    column,
    part_out,
    stat_out,
    send,
    recv,
    near_send,
    near_recv,
    merge_send,
    merge_recv,
    local,
):
    X, YH, YL, Z = sizes_of(blocks, heads)
    Y = YH * YL
    me, t = lax.axis_index("blk"), lax.axis_index("tensor")
    yl, z, c = me // (2 * Z), (me // 2) % Z, me % 2
    x, yh = t // YH, t % YH
    y = yh * YL + yl
    mine = yl * Z + z
    chips = YL * Z

    def dev(x, y, z, c):
        return ((y % YL) * (2 * Z) + z * 2 + c, x * YH + y // YL)

    axes = {
        "x": (X, x, lambda way: dev((x + way + X) % X, y, z, c)),
        "y": (Y, y, lambda way: dev(x, (y + way + Y) % Y, z, c)),
        "z": (Z, z, lambda way: dev(x, y, (z + way + Z) % Z, c)),
        "yl": (YL, yl, lambda way: dev(x, yh * YL + (1 - yl), z, c)),
        "yh": (YH, yh, lambda way: dev(x, (1 - yh) * YL + yl, z, c)),
    }
    sibling = dev(x, y, z, 1 - c)
    every = slice(None)
    rows = a_key.shape[0]
    cut = rows * 3 // 4
    upper, lower = pl.ds(0, cut), pl.ds(cut, rows - cut)

    def a_views(arrays, lone):
        def views(done, axis, at, half):
            chosen = arrays
            zs = every if "z" in done else (at if axis == "z" else z)
            if half is not None:
                if len(arrays) == 2:
                    chosen = arrays[half:half + 1]
                elif "z" in done:
                    zs = pl.ds(half * (Z // 2), Z // 2)
                elif half != lone:
                    chosen = []
            xs = every if "x" in done else (at if axis == "x" else x)
            if "y" in done:
                yls, yhs = every, every
            elif axis == "y":
                yls, yhs = at % YL, at // YL
            else:
                yls, yhs = yl, yh
            return [lambda a=a, r=r: a.at[yls, zs, c, xs, yhs, r] for a, r in chosen]

        return views

    def near_views(done, axis, at, half):
        chosen = [k_all, v_all] if half is None else [k_all, v_all][half:half + 1]
        return [lambda a=a: a.at[yh, at] for a in chosen]

    def far_views(done, axis, at, half):
        chosen = [k_all, v_all] if half is None else [k_all, v_all][half:half + 1]
        if axis == "yh":
            return [lambda a=a: a.at[at, x] for a in chosen]
        return [lambda a=a: a.at[1 - yh, at] for a in chosen]

    def query_views(done, axis, at, half):
        if half == 1:
            return []
        yls = every if "yl" in done else (at if axis == "yl" else yl)
        zs = at if axis == "z" else z
        return [lambda: q_all.at[yls, zs, c]]

    book = Book(send, recv)
    near = Gather(book, near_views, ["x"], axes, None)
    far = Gather(book, far_views, ["yh", "x"], axes, None)
    asked = Gather(book, query_views, ["yl", "z"], axes, sibling)
    piece_x = Gather(book, a_views([(key_all, upper)], 0), ["z*", "y", "x"], axes, sibling)
    piece_y = Gather(book, a_views([(value_all, upper)], 1), ["z*", "x", "y"], axes, sibling)
    piece_z = Gather(
        book, a_views([(key_all, lower), (value_all, lower)], 0), ["x*", "y*", "z"], axes, sibling
    )

    fresh = b_query.shape[0]
    count = k_all.shape[1] * k_all.shape[2]
    locals_ = [
        (cache_key, k_all.at[yh, x]),
        (cache_value, v_all.at[yh, x]),
        (b_query, q_all.at[yl, z, c]),
        (a_key, key_all.at[yl, z, c, x, yh]),
        (a_value, value_all.at[yl, z, c, x, yh]),
        (b_key, k_buf.at[pl.ds(count, fresh)]),
        (b_value, v_buf.at[pl.ds(count, fresh), pl.ds(0, HD)]),
        (lengths_hbm, lengths),
        (positions_hbm, positions),
    ]
    locals_ = [
        pltpu.make_async_copy(a, b, local.at[i]) for i, (a, b) in enumerate(locals_)
    ]
    for copy in locals_:
        copy.start()

    barrier = pltpu.get_barrier_semaphore()
    others = [dev((x + r) % X, y, z, c) for r in range(1, X)] + [
        dev(x, (1 - yh) * YL + yl, z, c),
        dev(x, (1 - yh) * YL + 1 - yl, z, c),
        sibling,
    ]
    for other in others:
        pl.semaphore_signal(barrier, inc=1, device_id=other, device_id_type=MESH)

    def greet(r, unused):
        pl.semaphore_signal(
            barrier, inc=1, device_id=((me + 2 * r) % blocks, t), device_id_type=MESH
        )
        return unused

    lax.fori_loop(1, chips, greet, 0)
    pl.semaphore_wait(barrier, len(others) + chips - 1)
    for copy in locals_[:-1]:
        copy.wait()

    far.run(0)
    near.run(0)
    asked.run(0)
    piece_z.run(0)
    piece_x.run(0)
    piece_y.run(0)
    column[...] = jnp.zeros(column.shape, jnp.float32)
    k_buf[count + fresh:, :] = jnp.zeros((HD - fresh, HD), jnp.bfloat16)
    v_buf[count + fresh:, :HD] = jnp.zeros((HD - fresh, HD), jnp.bfloat16)
    v_buf[count:, HD:] = jnp.ones((HD, HD), jnp.bfloat16)
    asked.run(1)
    piece_z.run(1)
    piece_x.run(1)
    piece_y.run(1)
    near.run(1)
    asked.run(2)
    piece_z.run(2)
    far.run(1)
    near.run(2)
    slots = k_all.shape[2]
    side = X * slots
    limit = lengths[me]

    def prepare(which, lead):
        row = lax.broadcasted_iota(jnp.int32, (side, HD), 0)
        live = (row // slots) * (YH * slots) + row % slots + which * slots < limit
        keys = k_all[which].reshape(side, HD).astype(jnp.float32)
        values = v_all[which].reshape(side, HD).astype(jnp.float32)
        lead = jnp.broadcast_to(lead, (side, HD))
        k_buf[:side, :] = jnp.where(live, keys, lead).astype(jnp.bfloat16)
        v_buf[:side, :HD] = jnp.where(live, values, 0.0).astype(jnp.bfloat16)
        v_buf[:side, HD:] = jnp.where(live, 1.0, 0.0).astype(jnp.bfloat16)

    prepare(yh, k_all[yh, 0][:1].astype(jnp.float32))
    asked.siblings(0, 3)

    tiles = blocks // OWNERS
    mine_tile = OWNERS // 2
    tile_rows = OWNERS * fresh
    soon = [
        (0, lambda: asked.run(3)),
        (0, lambda: piece_x.run(2)),
        (0, lambda: piece_y.run(2)),
        (1, lambda: asked.run(4)),
        (1, lambda: piece_z.run(3)),
        (1, lambda: far.run(2)),
        (1, lambda: asked.siblings(3, 5)),
        (2, lambda: piece_x.run(3)),
        (2, lambda: piece_y.run(3)),
        (2, lambda: asked.run(5)),
        (3, lambda: piece_z.run(4)),
        (3, lambda: asked.siblings(5)),
    ]
    late = [
        (0, lambda: piece_z.run(5)),
        (2, lambda: piece_z.run(6)),
        (2, lambda: piece_x.run(4)),
        (2, lambda: piece_y.run(4)),
    ]

    def serve(i, todo):
        for when, act in todo:
            if min(when, tiles - 1) == i:
                act()

    def tile_of(i):
        pairs = Z // 2
        away = ((i + 1) // 2) * (2 * (i % 2) - 1)
        return ((z // 2 + away + pairs) % pairs) * 2

    def queries_of(i):
        return jnp.concatenate(
            [
                q_all[yl_at, pl.ds(tile_of(i), 2)].reshape(tile_rows // 2, 2 * HD)
                for yl_at in range(YL)
            ],
            axis=0,
        )

    def near_copies(i):
        return [
            pltpu.make_async_remote_copy(
                src_ref=a.at[i, 1 - c],
                dst_ref=b.at[i],
                send_sem=near_send.at[n, i],
                recv_sem=near_recv.at[n, i],
                device_id=sibling,
                device_id_type=MESH,
            )
            for n, (a, b) in enumerate(((part, part_near), (col, col_near)))
        ]

    def merge_copies(source, slot, owner, sem):
        return [
            pltpu.make_async_remote_copy(
                src_ref=a,
                dst_ref=b.at[slot],
                send_sem=merge_send.at[n, sem],
                recv_sem=merge_recv.at[n, slot],
                device_id=(owner, t),
                device_id_type=MESH,
            )
            for n, (a, b) in enumerate(
                ((part_out.at[source], part_in), (stat_out.at[source // 2], stat_in))
            )
        ]

    def own_copies(source):
        return [
            pltpu.make_async_copy(a, b.at[mine], local.at[n])
            for n, (a, b) in enumerate(
                ((part_out.at[source], part_in), (stat_out.at[source // 2], stat_in))
            )
        ]

    half_rows = mine_tile * fresh
    lane = lax.broadcasted_iota(jnp.int32, (half_rows, HD), 1)

    def weigh(i):
        ours = col[i, c].reshape(half_rows, HD)
        theirs = col_near[i].reshape(half_rows, HD)
        stats, merged = [], []
        for h in range(2):
            base0, base1 = ours[:, h:h + 1], theirs[:, h:h + 1]
            base = jnp.maximum(base0, base1)
            share0 = ours[:, 2 + h:3 + h] * jnp.exp2(base0 - base)
            share1 = theirs[:, 2 + h:3 + h] * jnp.exp2(base1 - base)
            total = share0 + share1
            at = slice(h * HD, (h + 1) * HD)
            both = share0 * part[i, c, :, :, at].reshape(half_rows, HD).astype(
                jnp.float32
            ) + share1 * part_near[i, :, :, at].reshape(half_rows, HD).astype(jnp.float32)
            merged.append((both / total).astype(jnp.bfloat16))
            stats += [base, total]
        packed = jnp.where(
            lane == 0,
            stats[0],
            jnp.where(lane == 1, stats[2], jnp.where(lane == 2, stats[1], stats[3])),
        )
        for j in range(mine_tile):
            rows_j = slice(j * fresh, (j + 1) * fresh)
            for h in range(2):
                part_out[mine_tile * i + j, :, h * HD:(h + 1) * HD] = merged[h][rows_j]
            column[j * (HD // 2):j * (HD // 2) + fresh, :] = packed[rows_j]
        for n in range(YL):
            stat_out[YL * i + n] = column[n * HD:(n + 1) * HD, :].T[:8]

    def deliver(i):
        for j in range(mine_tile):
            slot = (j // 2) * Z + tile_of(i) + j % 2
            owner = 2 * slot + c

            def away():
                for copy in merge_copies(mine_tile * i + j, mine, owner, slot):
                    copy.start()

            if i > 0:
                away()
                continue

            pl.when(owner != me)(away)

            @pl.when(owner == me)
            def _():
                for copy in own_copies(j):
                    copy.start()

    wide = lax.broadcasted_iota(jnp.int32, (tile_rows, HD), 1)

    def pack(bases, sums):
        return jnp.where(
            wide == 0, bases[0], jnp.where(wide == 1, bases[1], jnp.where(wide == 2, sums[0], sums[1]))
        )

    def near_step(i):
        serve(i, soon)

        q = queries_of(i)
        bases, sums = [], []
        both = [dot(q[:, h * HD:(h + 1) * HD], k_buf[:side, :], NT) for h in range(2)]
        for h, scores in enumerate(both):
            base = jnp.max(scores, axis=1, keepdims=True) * SCALE2
            p = jnp.exp2(scores * SCALE2 - base).astype(jnp.bfloat16)
            acc = dot(p, v_buf[:side, :], NN)
            held[i, :, h * HD:(h + 1) * HD] = acc[:, :HD]
            bases.append(jnp.where(yh * slots < limit, base, LOWEST))
            sums.append(acc[:, HD:HD + 1])
        held_col[i] = pack(bases, sums)

    for i in range(tiles):
        near_step(i)
    far.run(3)
    locals_[-1].wait()

    def label(i, unused):
        order[i] = positions[i * BLOCK] // BLOCK
        return unused

    lax.fori_loop(0, order.shape[0], label, 0)
    prepare(1 - yh, k_all[0, 0][:1].astype(jnp.float32))

    def tile_step(i):
        serve(i, late)
        if i > 0:
            for copy in near_copies(i - 1):
                copy.wait_recv()

        q = queries_of(i)
        before = held_col[i]
        bases, sums, outs = [], [], []
        both = [
            (
                dot(q[:, h * HD:(h + 1) * HD], k_buf[:side, :], NT),
                dot(q[:, h * HD:(h + 1) * HD], k_buf[side:, :], NT),
            )
            for h in range(2)
        ]
        for h, (scores, extra) in enumerate(both):
            ki = lax.broadcasted_iota(jnp.int32, extra.shape, 1)
            ti = lax.broadcasted_iota(jnp.int32, extra.shape, 0)
            ti = ti + 2 * tile_of(i) * fresh + jnp.where(
                ti >= half_rows, 2 * Z * fresh - half_rows, 0
            )
            seen = jnp.logical_and(ki < fresh, ki + me * fresh <= ti)
            extra = jnp.where(seen, extra, LOWEST)
            top = jnp.maximum(
                jnp.max(scores, axis=1, keepdims=True), jnp.max(extra, axis=1, keepdims=True)
            )
            old = before[:, h:h + 1]
            base = jnp.maximum(old, top * SCALE2)
            factor = jnp.exp2(old - base)
            p = jnp.exp2(scores * SCALE2 - base).astype(jnp.bfloat16)
            p_extra = jnp.exp2(extra * SCALE2 - base).astype(jnp.bfloat16)
            acc = dot(p, v_buf[:side, :], NN) + dot(p_extra, v_buf[side:, :], NN)
            total = acc[:, HD:HD + 1] + before[:, 2 + h:3 + h] * factor
            outs.append(
                ((acc[:, :HD] + held[i, :, h * HD:(h + 1) * HD] * factor) / total).astype(
                    jnp.bfloat16
                )
            )
            bases.append(base)
            sums.append(total)
        packed = pack(bases, sums)
        for j in range(OWNERS):
            at = slice(j * fresh, (j + 1) * fresh)
            for h in range(2):
                part[i, j % 2, j // 2, :, h * HD:(h + 1) * HD] = outs[h][at]
            col[i, j % 2, j // 2] = packed[at]
        if i > 0:
            weigh(i - 1)
        for copy in near_copies(i):
            copy.start()
        if i > 0:
            deliver(i - 1)

    for i in range(tiles):
        tile_step(i)
    for copy in near_copies(tiles - 1):
        copy.wait_recv()
    weigh(tiles - 1)
    deliver(tiles - 1)
    piece_x.run(5)
    piece_y.run(5)
    for copy in own_copies(0):
        copy.wait()

    def arrive(r, unused):
        other = (mine + r) % chips
        for copy in merge_copies(0, other, 2 * other + c, other):
            copy.wait_recv()
        return unused

    lax.fori_loop(1, chips, arrive, 0)
    for piece in (piece_x, piece_y, piece_z):
        piece.siblings()
    for copy in book.copies:
        copy.make().wait_send()

    def leave(r, unused):
        other = (mine + r) % chips
        for copy in merge_copies(0, other, 2 * other + c, other):
            copy.wait_send()
        return unused

    lax.fori_loop(1, chips, leave, 0)

    def part_ways(i, unused):
        for copy in near_copies(i):
            copy.wait_send()
        return unused

    lax.fori_loop(0, tiles, part_ways, 0)


def exchange(blocks, heads, lengths, positions, a_key, a_value, b_query, b_key, b_value, cache_key, cache_value):
    X, YH, YL, Z = sizes_of(blocks, heads)
    rows = a_key.shape[0]
    fresh = b_query.shape[0]
    slots = cache_key.shape[0]
    count = slots * X
    chips = YL * Z
    tiles = blocks // OWNERS
    half = OWNERS // 2
    whole = jax.ShapeDtypeStruct((YL, Z, 2, X, YH, rows, HD), jnp.bfloat16)
    hbm = pl.BlockSpec(memory_space=pltpu.HBM)
    anywhere = pl.BlockSpec(memory_space=pl.ANY)
    copies = 128
    return pl.pallas_call(
        functools.partial(exchange_kernel, blocks, heads),
        out_shape=(
            whole,
            whole,
            jax.ShapeDtypeStruct((chips, fresh, 2 * HD), jnp.bfloat16),
            jax.ShapeDtypeStruct((chips, 8, HD), jnp.float32),
            jax.ShapeDtypeStruct((positions.shape[0] // BLOCK,), jnp.int32),
        ),
        in_specs=[hbm] * 9,
        out_specs=[anywhere] * 4 + [pl.BlockSpec(memory_space=pltpu.SMEM)],
        scratch_shapes=[
            pltpu.SMEM(lengths.shape, jnp.int32),
            pltpu.SMEM(positions.shape, jnp.int32),
            pltpu.VMEM((YL, Z, 2, fresh, 2 * HD), jnp.bfloat16),
            pltpu.VMEM((YH, X, slots, HD), jnp.bfloat16),
            pltpu.VMEM((YH, X, slots, HD), jnp.bfloat16),
            pltpu.VMEM((count + HD, HD), jnp.bfloat16),
            pltpu.VMEM((count + HD, 2 * HD), jnp.bfloat16),
            pltpu.VMEM((tiles, 2, half, fresh, 2 * HD), jnp.bfloat16),
            pltpu.VMEM((tiles, 2, half, fresh, HD), jnp.float32),
            pltpu.VMEM((tiles, half, fresh, 2 * HD), jnp.bfloat16),
            pltpu.VMEM((tiles, half, fresh, HD), jnp.float32),
            pltpu.VMEM((tiles, OWNERS * fresh, 2 * HD), jnp.float32),
            pltpu.VMEM((tiles, OWNERS * fresh, HD), jnp.float32),
            pltpu.VMEM((2 * HD, HD), jnp.float32),
            pltpu.VMEM((chips, fresh, 2 * HD), jnp.bfloat16),
            pltpu.VMEM((YL * tiles, 8, HD), jnp.float32),
            pltpu.SemaphoreType.DMA((copies,)),
            pltpu.SemaphoreType.DMA((copies,)),
            pltpu.SemaphoreType.DMA((2, tiles)),
            pltpu.SemaphoreType.DMA((2, tiles)),
            pltpu.SemaphoreType.DMA((2, chips)),
            pltpu.SemaphoreType.DMA((2, chips)),
            pltpu.SemaphoreType.DMA((9,)),
        ],
        compiler_params=pltpu.CompilerParams(
            vmem_limit_bytes=32 * 2**20, collective_id=0, has_side_effects=True
        ),
        cost_estimate=pl.CostEstimate(
            flops=10_000_000_000, bytes_accessed=20_000_000, transcendentals=6_700_000
        ),
        name="exchange",
    )(
        *[
            pltpu.with_memory_space_constraint(v, pltpu.HBM)
            for v in (
                lengths, positions, a_key, a_value, b_query, b_key, b_value, cache_key, cache_value
            )
        ]
    )


def a_kernel(
    fresh, pos_ref, q_ref, key_ref, value_ref, part_ref, stat_ref, o_ref, b_ref,
    q_buf, s_buf, m_buf, acc_buf, place,
):
    total = key_ref.shape[0]
    chips = part_ref.shape[0]
    group = lax.axis_index("blk")
    own = [pos_ref[2 * group], pos_ref[2 * group + 1]]
    wholes = own[0] // CHUNK
    steps = total // CHUNK - 1
    unroll = 5 if steps % 5 == 0 else 1

    def invert(i, unused):
        place[pos_ref[i]] = i
        return unused

    lax.fori_loop(0, total, invert, 0)
    ones = jnp.ones((CHUNK * BLOCK, HD), jnp.bfloat16)
    for part in range(2):
        for h in range(2):
            q = q_ref[part * BLOCK:(part + 1) * BLOCK, h * HD:(h + 1) * HD]
            q = q.astype(jnp.float32) * SCALE2
            main = q.astype(jnp.bfloat16)
            q_buf[part, h, :, :HD] = main
            q_buf[part, h, :, HD:] = (q - main.astype(jnp.float32)).astype(jnp.bfloat16)

    def load_keys(at):
        keys = jnp.concatenate([key_ref[place[at * CHUNK + b]] for b in range(CHUNK)], axis=0)
        return jnp.concatenate([keys, keys], axis=1)

    def load_values(at):
        values = jnp.concatenate([value_ref[place[at * CHUNK + b]] for b in range(CHUNK)], axis=0)
        return jnp.concatenate([values, ones], axis=1)

    for part in range(2):
        at = own[part] // CHUNK
        keys, values = load_keys(at), load_values(at)
        for h in range(2):
            s = dot(q_buf[part, h], keys, NT)
            ki = lax.broadcasted_iota(jnp.int32, s.shape, 1) + (at * CHUNK - own[part]) * BLOCK
            qi = lax.broadcasted_iota(jnp.int32, s.shape, 0)
            s = jnp.where(ki <= qi, s, LOWEST)
            new = jnp.max(s, axis=1, keepdims=True)
            m_buf[part, h] = jnp.broadcast_to(new, (BLOCK, HD))
            p = jnp.exp2(s - new).astype(jnp.bfloat16)
            acc_buf[part, h] = dot(p, values, NN)

    def place_of(i):
        i = jnp.minimum(i, steps - 1)
        part = (i >= wholes).astype(jnp.int32)
        return part, i - part * wholes

    def score(i, h):
        part, at = place_of(i)
        return dot(q_buf[part, h], load_keys(at), NT)

    s_buf[...] = score(0, 0)

    def step(j, unused):
        ready = s_buf[...]
        for n in range(unroll):
            i = j * unroll + n
            part, at = place_of(i)
            values = load_values(at)
            for h in range(2):
                s = ready
                ready = score(i + h, 1 - h)
                old = m_buf[part, h]
                new = jnp.maximum(old, jnp.max(s, axis=1, keepdims=True))
                m_buf[part, h] = new
                factor = jnp.exp2(old - new)
                p = jnp.exp2(s - new[:, :1]).astype(jnp.bfloat16)
                acc_buf[part, h] = acc_buf[part, h] * factor[:, :1] + dot(p, values, NN)
        s_buf[...] = ready
        return unused

    lax.fori_loop(0, steps // unroll, step, 0)
    for part in range(2):
        for h in range(2):
            acc = acc_buf[part, h]
            o_ref[part * BLOCK:(part + 1) * BLOCK, h * HD:(h + 1) * HD] = (
                acc[:, :HD] / acc[:, HD:]
            ).astype(jnp.bfloat16)

    odd = (group // 2) % 2 == 1
    for h in range(2):
        base = stat_ref[:, h, :]
        best = jnp.max(base, axis=0, keepdims=True)
        share = stat_ref[:, 2 + h, :] * jnp.exp2(base - best)
        share = jnp.concatenate(
            [share, jnp.zeros((HD - chips, HD), jnp.float32)], axis=0
        ).T
        share = jnp.where(odd, share[HD // 2:HD // 2 + fresh], share[:fresh])
        numer = jnp.zeros((fresh, HD), jnp.float32)
        for g in range(chips):
            numer = numer + share[:, g:g + 1] * part_ref[g, :, h * HD:(h + 1) * HD].astype(
                jnp.float32
            )
        denom = jnp.sum(share, axis=1, keepdims=True)
        b_ref[:, h * HD:(h + 1) * HD] = (numer / denom).astype(jnp.bfloat16)


def attend_a(fresh, positions, queries, keys, values, part, stat):
    total = positions.shape[0]
    vmem = pl.BlockSpec(memory_space=pltpu.VMEM)
    return pl.pallas_call(
        functools.partial(a_kernel, fresh),
        out_shape=(
            jax.ShapeDtypeStruct(queries.shape, jnp.bfloat16),
            jax.ShapeDtypeStruct((fresh, 2 * HD), jnp.bfloat16),
        ),
        in_specs=[pl.BlockSpec(memory_space=pltpu.SMEM)] + [vmem] * 5,
        out_specs=[vmem, vmem],
        scratch_shapes=[
            pltpu.VMEM((2, 2, BLOCK, 2 * HD), jnp.bfloat16),
            pltpu.VMEM((BLOCK, CHUNK * BLOCK), jnp.float32),
            pltpu.VMEM((2, 2, BLOCK, HD), jnp.float32),
            pltpu.VMEM((2, 2, BLOCK, 2 * HD), jnp.float32),
            pltpu.SMEM((total,), jnp.int32),
        ],
        compiler_params=pltpu.CompilerParams(vmem_limit_bytes=32 * 2**20),
        cost_estimate=pl.CostEstimate(
            flops=10_000_000_000, bytes_accessed=9_000_000, transcendentals=8_500_000
        ),
        name="attend_a",
    )(positions, queries, keys.reshape(total, -1, HD), values.reshape(total, -1, HD), part, stat)


def shards(
    blocks,
    heads,
    a_query,
    a_key,
    a_value,
    b_query,
    b_key,
    b_value,
    cache_key,
    cache_value,
    a_positions,
    cache_lengths,
):
    *gathered, order = exchange(
        blocks,
        heads,
        cache_lengths,
        a_positions,
        a_key,
        a_value,
        b_query,
        b_key,
        b_value,
        cache_key,
        cache_value,
    )
    return attend_a(b_query.shape[0], order, a_query, *gathered)


def solution(mesh):
    in_specs = (
        P("blk", "tensor"),
        P(("blk", "tensor"), None),
        P(("blk", "tensor"), None),
        P("blk", "tensor"),
        P("blk", None),
        P("blk", None),
        P(("blk", "tensor"), None),
        P(("blk", "tensor"), None),
        P(),
        P(),
    )
    out_specs = (P("blk", "tensor"), P("blk", "tensor"))
    body = functools.partial(shards, mesh.shape["blk"], mesh.shape["tensor"])
    return jax.shard_map(body, mesh=mesh, in_specs=in_specs, out_specs=out_specs, check_vma=False)
```

```python
import functools
import math

import jax
import jax.numpy as jnp
from jax import lax
from jax.experimental import pallas as pl
from jax.experimental.pallas import tpu as pltpu
from jax.sharding import PartitionSpec as P

HD = 128
BLOCK = 256
CHUNK = 4
OWNERS = 8
SCALE2 = HD ** (-0.5) * math.log2(math.e)
LOWEST = -1e30
NT = (((1,), (1,)), ((), ()))
NN = (((1,), (0,)), ((), ()))
MESH = pl.DeviceIdType.MESH


def dot(a, b, dims):
    return lax.dot_general(a, b, dims, preferred_element_type=jnp.float32)


class Copy:
    def __init__(self, book, view, device):
        self.book, self.view, self.device = book, view, device
        self.index = len(book.copies)
        book.copies.append(self)

    def make(self):
        return pltpu.make_async_remote_copy(
            src_ref=self.view(),
            dst_ref=self.view(),
            send_sem=self.book.send.at[self.index],
            recv_sem=self.book.recv.at[self.index],
            device_id=self.device,
            device_id_type=MESH,
        )


class Book:
    def __init__(self, send, recv):
        self.send, self.recv, self.copies = send, recv, []


class Gather:
    def __init__(self, book, views, order, axes, sibling):
        self.steps, self.forwards = [], []
        done = []
        for number, name in enumerate(order):
            axis = name.rstrip("*")
            size, at, device = axes[axis]
            final = number == len(order) - 1 and sibling is not None
            if final:
                self.forwards = [[] for step in self.steps]
                self.forwards.append(
                    [Copy(book, v, sibling) for v in views(tuple(done), axis, at, None)]
                )
            if name.endswith("*"):
                sends = []
                for way in range(1, size):
                    for v in views(tuple(done), axis, at, None):
                        sends.append(Copy(book, v, device(way)))
                if sends:
                    self.steps.append(sends)
                done.append(axis)
                continue
            for k in range(1, size // 2 + 1):
                sends, arrived = [], []
                for way in (1, -1):
                    if size == 2 and way == -1:
                        continue
                    half = None
                    if 2 * k == size and size > 2:
                        half = 0 if way == 1 else 1
                    out = (at - way * (k - 1) + 2 * size) % size
                    got = (at - way * k + 2 * size) % size
                    for v in views(tuple(done), axis, out, half):
                        sends.append(Copy(book, v, device(way)))
                    if final:
                        for v in views(tuple(done), axis, got, half):
                            arrived.append(Copy(book, v, sibling))
                self.steps.append(sends)
                if final:
                    self.forwards.append(arrived)
            done.append(axis)

    def run(self, step):
        if step > len(self.steps):
            return
        if step > 0:
            for copy in self.steps[step - 1]:
                copy.make().wait_recv()
        if step < len(self.steps):
            for copy in self.steps[step]:
                copy.make().start()
        if step < len(self.forwards):
            for copy in self.forwards[step]:
                copy.make().start()

    def siblings(self, first=0, last=99):
        for group in self.forwards[first:last]:
            for copy in group:
                copy.make().wait_recv()


def sizes_of(blocks, heads):
    y_lo, y_hi = 2, 2
    return heads // y_hi, y_hi, y_lo, blocks // (2 * y_lo)


def exchange_kernel(
    blocks,
    heads,
    lengths_hbm,
    positions_hbm,
    a_key,
    a_value,
    b_query,
    b_key,
    b_value,
    cache_key,
    cache_value,
    key_all,
    value_all,
    part_in,
    stat_in,
    order,
    lengths,
    positions,
    q_all,
    k_all,
    v_all,
    k_buf,
    v_buf,
    part,
    col,
    part_near,
    col_near,
    held,
    held_col,
    column,
    part_out,
    stat_out,
    send,
    recv,
    near_send,
    near_recv,
    merge_send,
    merge_recv,
    local,
):
    X, YH, YL, Z = sizes_of(blocks, heads)
    Y = YH * YL
    me, t = lax.axis_index("blk"), lax.axis_index("tensor")
    yl, z, c = me // (2 * Z), (me // 2) % Z, me % 2
    x, yh = t // YH, t % YH
    y = yh * YL + yl
    mine = yl * Z + z
    chips = YL * Z

    def dev(x, y, z, c):
        return ((y % YL) * (2 * Z) + z * 2 + c, x * YH + y // YL)

    axes = {
        "x": (X, x, lambda way: dev((x + way + X) % X, y, z, c)),
        "y": (Y, y, lambda way: dev(x, (y + way + Y) % Y, z, c)),
        "z": (Z, z, lambda way: dev(x, y, (z + way + Z) % Z, c)),
        "yl": (YL, yl, lambda way: dev(x, yh * YL + (1 - yl), z, c)),
        "yh": (YH, yh, lambda way: dev(x, (1 - yh) * YL + yl, z, c)),
    }
    sibling = dev(x, y, z, 1 - c)
    every = slice(None)
    rows = a_key.shape[0]
    cut = rows * 3 // 4
    upper, lower = pl.ds(0, cut), pl.ds(cut, rows - cut)

    def a_views(arrays, lone):
        def views(done, axis, at, half):
            chosen = arrays
            zs = every if "z" in done else (at if axis == "z" else z)
            if half is not None:
                if len(arrays) == 2:
                    chosen = arrays[half:half + 1]
                elif "z" in done:
                    zs = pl.ds(half * (Z // 2), Z // 2)
                elif half != lone:
                    chosen = []
            xs = every if "x" in done else (at if axis == "x" else x)
            if "y" in done:
                yls, yhs = every, every
            elif axis == "y":
                yls, yhs = at % YL, at // YL
            else:
                yls, yhs = yl, yh
            return [lambda a=a, r=r: a.at[yls, zs, c, xs, yhs, r] for a, r in chosen]

        return views

    def near_views(done, axis, at, half):
        chosen = [k_all, v_all] if half is None else [k_all, v_all][half:half + 1]
        return [lambda a=a: a.at[yh, at] for a in chosen]

    def far_views(done, axis, at, half):
        chosen = [k_all, v_all] if half is None else [k_all, v_all][half:half + 1]
        if axis == "yh":
            return [lambda a=a: a.at[at, x] for a in chosen]
        return [lambda a=a: a.at[1 - yh, at] for a in chosen]

    def query_views(done, axis, at, half):
        if half == 1:
            return []
        yls = every if "yl" in done else (at if axis == "yl" else yl)
        zs = at if axis == "z" else z
        return [lambda: q_all.at[yls, zs, c]]

    book = Book(send, recv)
    near = Gather(book, near_views, ["x"], axes, None)
    far = Gather(book, far_views, ["yh", "x"], axes, None)
    asked = Gather(book, query_views, ["yl", "z"], axes, sibling)
    piece_x = Gather(book, a_views([(key_all, upper)], 0), ["z*", "y", "x"], axes, sibling)
    piece_y = Gather(book, a_views([(value_all, upper)], 1), ["z*", "x", "y"], axes, sibling)
    piece_z = Gather(
        book, a_views([(key_all, lower), (value_all, lower)], 0), ["x*", "y*", "z"], axes, sibling
    )

    fresh = b_query.shape[0]
    count = k_all.shape[1] * k_all.shape[2]
    locals_ = [
        (cache_key, k_all.at[yh, x]),
        (cache_value, v_all.at[yh, x]),
        (b_query, q_all.at[yl, z, c]),
        (a_key, key_all.at[yl, z, c, x, yh]),
        (a_value, value_all.at[yl, z, c, x, yh]),
        (b_key, k_buf.at[pl.ds(count, fresh)]),
        (b_value, v_buf.at[pl.ds(count, fresh), pl.ds(0, HD)]),
        (lengths_hbm, lengths),
        (positions_hbm, positions),
    ]
    locals_ = [
        pltpu.make_async_copy(a, b, local.at[i]) for i, (a, b) in enumerate(locals_)
    ]
    for copy in locals_:
        copy.start()

    barrier = pltpu.get_barrier_semaphore()
    others = [dev((x + r) % X, y, z, c) for r in range(1, X)] + [
        dev(x, (1 - yh) * YL + yl, z, c),
        dev(x, (1 - yh) * YL + 1 - yl, z, c),
        sibling,
    ]
    for other in others:
        pl.semaphore_signal(barrier, inc=1, device_id=other, device_id_type=MESH)

    def greet(r, unused):
        pl.semaphore_signal(
            barrier, inc=1, device_id=((me + 2 * r) % blocks, t), device_id_type=MESH
        )
        return unused

    lax.fori_loop(1, chips, greet, 0)
    pl.semaphore_wait(barrier, len(others) + chips - 1)
    for copy in locals_[:-1]:
        copy.wait()

    far.run(0)
    near.run(0)
    asked.run(0)
    piece_z.run(0)
    piece_x.run(0)
    piece_y.run(0)
    column[...] = jnp.zeros(column.shape, jnp.float32)
    k_buf[count + fresh:, :] = jnp.zeros((HD - fresh, HD), jnp.bfloat16)
    v_buf[count + fresh:, :HD] = jnp.zeros((HD - fresh, HD), jnp.bfloat16)
    v_buf[count:, HD:] = jnp.ones((HD, HD), jnp.bfloat16)
    asked.run(1)
    piece_z.run(1)
    piece_x.run(1)
    piece_y.run(1)
    near.run(1)
    asked.run(2)
    piece_z.run(2)
    far.run(1)
    near.run(2)
    slots = k_all.shape[2]
    side = X * slots
    limit = lengths[me]

    def prepare(which, lead):
        row = lax.broadcasted_iota(jnp.int32, (side, HD), 0)
        live = (row // slots) * (YH * slots) + row % slots + which * slots < limit
        keys = k_all[which].reshape(side, HD).astype(jnp.float32)
        values = v_all[which].reshape(side, HD).astype(jnp.float32)
        lead = jnp.broadcast_to(lead, (side, HD))
        k_buf[:side, :] = jnp.where(live, keys, lead).astype(jnp.bfloat16)
        v_buf[:side, :HD] = jnp.where(live, values, 0.0).astype(jnp.bfloat16)
        v_buf[:side, HD:] = jnp.where(live, 1.0, 0.0).astype(jnp.bfloat16)

    prepare(yh, k_all[yh, 0][:1].astype(jnp.float32))
    asked.siblings(0, 3)

    tiles = blocks // OWNERS
    mine_tile = OWNERS // 2
    tile_rows = OWNERS * fresh
    soon = [
        (0, lambda: asked.run(3)),
        (0, lambda: piece_x.run(2)),
        (0, lambda: piece_y.run(2)),
        (1, lambda: asked.run(4)),
        (1, lambda: far.run(2)),
        (1, lambda: piece_x.run(3)),
        (1, lambda: piece_y.run(3)),
        (1, lambda: piece_z.run(3)),
        (1, lambda: asked.siblings(3, 5)),
        (2, lambda: asked.run(5)),
        (2, lambda: piece_z.run(4)),
        (3, lambda: piece_z.run(5)),
        (3, lambda: asked.siblings(5)),
    ]
    late = [
        (0, lambda: piece_z.run(6)),
        (2, lambda: piece_x.run(4)),
        (2, lambda: piece_y.run(4)),
    ]

    def serve(i, todo):
        for when, act in todo:
            if min(when, tiles - 1) == i:
                act()

    def tile_of(i):
        pairs = Z // 2
        away = ((i + 1) // 2) * (2 * (i % 2) - 1)
        return ((z // 2 + away + pairs) % pairs) * 2

    def queries_of(i):
        return jnp.concatenate(
            [
                q_all[yl_at, pl.ds(tile_of(i), 2)].reshape(tile_rows // 2, 2 * HD)
                for yl_at in range(YL)
            ],
            axis=0,
        )

    def near_copies(i):
        return [
            pltpu.make_async_remote_copy(
                src_ref=a.at[i, 1 - c],
                dst_ref=b.at[i],
                send_sem=near_send.at[n, i],
                recv_sem=near_recv.at[n, i],
                device_id=sibling,
                device_id_type=MESH,
            )
            for n, (a, b) in enumerate(((part, part_near), (col, col_near)))
        ]

    def merge_copies(source, slot, owner, sem):
        return [
            pltpu.make_async_remote_copy(
                src_ref=a,
                dst_ref=b.at[slot],
                send_sem=merge_send.at[n, sem],
                recv_sem=merge_recv.at[n, slot],
                device_id=(owner, t),
                device_id_type=MESH,
            )
            for n, (a, b) in enumerate(
                ((part_out.at[source], part_in), (stat_out.at[source // 2], stat_in))
            )
        ]

    def own_copies(source):
        return [
            pltpu.make_async_copy(a, b.at[mine], local.at[n])
            for n, (a, b) in enumerate(
                ((part_out.at[source], part_in), (stat_out.at[source // 2], stat_in))
            )
        ]

    half_rows = mine_tile * fresh
    lane = lax.broadcasted_iota(jnp.int32, (half_rows, HD), 1)

    def weigh(i):
        ours = col[i, c].reshape(half_rows, HD)
        theirs = col_near[i].reshape(half_rows, HD)
        stats, merged = [], []
        for h in range(2):
            base0, base1 = ours[:, h:h + 1], theirs[:, h:h + 1]
            base = jnp.maximum(base0, base1)
            share0 = ours[:, 2 + h:3 + h] * jnp.exp2(base0 - base)
            share1 = theirs[:, 2 + h:3 + h] * jnp.exp2(base1 - base)
            total = share0 + share1
            at = slice(h * HD, (h + 1) * HD)
            both = share0 * part[i, c, :, :, at].reshape(half_rows, HD).astype(
                jnp.float32
            ) + share1 * part_near[i, :, :, at].reshape(half_rows, HD).astype(jnp.float32)
            merged.append((both / total).astype(jnp.bfloat16))
            stats += [base, total]
        packed = jnp.where(
            lane == 0,
            stats[0],
            jnp.where(lane == 1, stats[2], jnp.where(lane == 2, stats[1], stats[3])),
        )
        for j in range(mine_tile):
            rows_j = slice(j * fresh, (j + 1) * fresh)
            for h in range(2):
                part_out[mine_tile * i + j, :, h * HD:(h + 1) * HD] = merged[h][rows_j]
            column[j * (HD // 2):j * (HD // 2) + fresh, :] = packed[rows_j]
        for n in range(YL):
            stat_out[YL * i + n] = column[n * HD:(n + 1) * HD, :].T[:8]

    def deliver(i):
        for j in range(mine_tile):
            slot = (j // 2) * Z + tile_of(i) + j % 2
            owner = 2 * slot + c

            def away():
                for copy in merge_copies(mine_tile * i + j, mine, owner, slot):
                    copy.start()

            if i > 0:
                away()
                continue

            pl.when(owner != me)(away)

            @pl.when(owner == me)
            def _():
                for copy in own_copies(j):
                    copy.start()

    wide = lax.broadcasted_iota(jnp.int32, (tile_rows, HD), 1)

    def pack(bases, sums):
        return jnp.where(
            wide == 0, bases[0], jnp.where(wide == 1, bases[1], jnp.where(wide == 2, sums[0], sums[1]))
        )

    def near_step(i):
        serve(i, soon)

        q = queries_of(i)
        bases, sums = [], []
        both = [dot(q[:, h * HD:(h + 1) * HD], k_buf[:side, :], NT) for h in range(2)]
        for h, scores in enumerate(both):
            base = jnp.max(scores, axis=1, keepdims=True) * SCALE2
            p = jnp.exp2(scores * SCALE2 - base).astype(jnp.bfloat16)
            acc = dot(p, v_buf[:side, :], NN)
            held[i, :, h * HD:(h + 1) * HD] = acc[:, :HD]
            bases.append(jnp.where(yh * slots < limit, base, LOWEST))
            sums.append(acc[:, HD:HD + 1])
        held_col[i] = pack(bases, sums)

    for i in range(tiles):
        near_step(i)
    far.run(3)
    locals_[-1].wait()

    def label(i, unused):
        order[i] = positions[i * BLOCK] // BLOCK
        return unused

    lax.fori_loop(0, order.shape[0], label, 0)
    prepare(1 - yh, k_all[0, 0][:1].astype(jnp.float32))

    def tile_step(i):
        serve(i, late)
        if i > 0:
            for copy in near_copies(i - 1):
                copy.wait_recv()

        q = queries_of(i)
        before = held_col[i]
        bases, sums, outs = [], [], []
        both = [
            (
                dot(q[:, h * HD:(h + 1) * HD], k_buf[:side, :], NT),
                dot(q[:, h * HD:(h + 1) * HD], k_buf[side:, :], NT),
            )
            for h in range(2)
        ]
        for h, (scores, extra) in enumerate(both):
            ki = lax.broadcasted_iota(jnp.int32, extra.shape, 1)
            ti = lax.broadcasted_iota(jnp.int32, extra.shape, 0)
            ti = ti + 2 * tile_of(i) * fresh + jnp.where(
                ti >= half_rows, 2 * Z * fresh - half_rows, 0
            )
            seen = jnp.logical_and(ki < fresh, ki + me * fresh <= ti)
            extra = jnp.where(seen, extra, LOWEST)
            top = jnp.maximum(
                jnp.max(scores, axis=1, keepdims=True), jnp.max(extra, axis=1, keepdims=True)
            )
            old = before[:, h:h + 1]
            base = jnp.maximum(old, top * SCALE2)
            factor = jnp.exp2(old - base)
            p = jnp.exp2(scores * SCALE2 - base).astype(jnp.bfloat16)
            p_extra = jnp.exp2(extra * SCALE2 - base).astype(jnp.bfloat16)
            acc = dot(p, v_buf[:side, :], NN) + dot(p_extra, v_buf[side:, :], NN)
            total = acc[:, HD:HD + 1] + before[:, 2 + h:3 + h] * factor
            outs.append(
                ((acc[:, :HD] + held[i, :, h * HD:(h + 1) * HD] * factor) / total).astype(
                    jnp.bfloat16
                )
            )
            bases.append(base)
            sums.append(total)
        packed = pack(bases, sums)
        for j in range(OWNERS):
            at = slice(j * fresh, (j + 1) * fresh)
            for h in range(2):
                part[i, j % 2, j // 2, :, h * HD:(h + 1) * HD] = outs[h][at]
            col[i, j % 2, j // 2] = packed[at]
        if i > 0:
            weigh(i - 1)
        for copy in near_copies(i):
            copy.start()
        if i > 0:
            deliver(i - 1)

    for i in range(tiles):
        tile_step(i)
    for copy in near_copies(tiles - 1):
        copy.wait_recv()
    weigh(tiles - 1)
    deliver(tiles - 1)
    piece_x.run(5)
    piece_y.run(5)
    for copy in own_copies(0):
        copy.wait()

    def arrive(r, unused):
        other = (mine + r) % chips
        for copy in merge_copies(0, other, 2 * other + c, other):
            copy.wait_recv()
        return unused

    lax.fori_loop(1, chips, arrive, 0)
    for piece in (piece_x, piece_y, piece_z):
        piece.siblings()
    for copy in book.copies:
        copy.make().wait_send()

    def leave(r, unused):
        other = (mine + r) % chips
        for copy in merge_copies(0, other, 2 * other + c, other):
            copy.wait_send()
        return unused

    lax.fori_loop(1, chips, leave, 0)

    def part_ways(i, unused):
        for copy in near_copies(i):
            copy.wait_send()
        return unused

    lax.fori_loop(0, tiles, part_ways, 0)


def exchange(blocks, heads, lengths, positions, a_key, a_value, b_query, b_key, b_value, cache_key, cache_value):
    X, YH, YL, Z = sizes_of(blocks, heads)
    rows = a_key.shape[0]
    fresh = b_query.shape[0]
    slots = cache_key.shape[0]
    count = slots * X
    chips = YL * Z
    tiles = blocks // OWNERS
    half = OWNERS // 2
    whole = jax.ShapeDtypeStruct((YL, Z, 2, X, YH, rows, HD), jnp.bfloat16)
    hbm = pl.BlockSpec(memory_space=pltpu.HBM)
    anywhere = pl.BlockSpec(memory_space=pl.ANY)
    copies = 128
    return pl.pallas_call(
        functools.partial(exchange_kernel, blocks, heads),
        out_shape=(
            whole,
            whole,
            jax.ShapeDtypeStruct((chips, fresh, 2 * HD), jnp.bfloat16),
            jax.ShapeDtypeStruct((chips, 8, HD), jnp.float32),
            jax.ShapeDtypeStruct((positions.shape[0] // BLOCK,), jnp.int32),
        ),
        in_specs=[hbm] * 9,
        out_specs=[anywhere] * 4 + [pl.BlockSpec(memory_space=pltpu.SMEM)],
        scratch_shapes=[
            pltpu.SMEM(lengths.shape, jnp.int32),
            pltpu.SMEM(positions.shape, jnp.int32),
            pltpu.VMEM((YL, Z, 2, fresh, 2 * HD), jnp.bfloat16),
            pltpu.VMEM((YH, X, slots, HD), jnp.bfloat16),
            pltpu.VMEM((YH, X, slots, HD), jnp.bfloat16),
            pltpu.VMEM((count + HD, HD), jnp.bfloat16),
            pltpu.VMEM((count + HD, 2 * HD), jnp.bfloat16),
            pltpu.VMEM((tiles, 2, half, fresh, 2 * HD), jnp.bfloat16),
            pltpu.VMEM((tiles, 2, half, fresh, HD), jnp.float32),
            pltpu.VMEM((tiles, half, fresh, 2 * HD), jnp.bfloat16),
            pltpu.VMEM((tiles, half, fresh, HD), jnp.float32),
            pltpu.VMEM((tiles, OWNERS * fresh, 2 * HD), jnp.float32),
            pltpu.VMEM((tiles, OWNERS * fresh, HD), jnp.float32),
            pltpu.VMEM((2 * HD, HD), jnp.float32),
            pltpu.VMEM((chips, fresh, 2 * HD), jnp.bfloat16),
            pltpu.VMEM((YL * tiles, 8, HD), jnp.float32),
            pltpu.SemaphoreType.DMA((copies,)),
            pltpu.SemaphoreType.DMA((copies,)),
            pltpu.SemaphoreType.DMA((2, tiles)),
            pltpu.SemaphoreType.DMA((2, tiles)),
            pltpu.SemaphoreType.DMA((2, chips)),
            pltpu.SemaphoreType.DMA((2, chips)),
            pltpu.SemaphoreType.DMA((9,)),
        ],
        compiler_params=pltpu.CompilerParams(
            vmem_limit_bytes=32 * 2**20, collective_id=0, has_side_effects=True
        ),
        cost_estimate=pl.CostEstimate(
            flops=10_000_000_000, bytes_accessed=20_000_000, transcendentals=6_700_000
        ),
        name="exchange",
    )(
        *[
            pltpu.with_memory_space_constraint(v, pltpu.HBM)
            for v in (
                lengths, positions, a_key, a_value, b_query, b_key, b_value, cache_key, cache_value
            )
        ]
    )


def a_kernel(
    fresh, pos_ref, q_ref, key_ref, value_ref, part_ref, stat_ref, o_ref, b_ref,
    q_buf, s_buf, m_buf, acc_buf, place,
):
    total = key_ref.shape[0]
    chips = part_ref.shape[0]
    group = lax.axis_index("blk")
    own = [pos_ref[2 * group], pos_ref[2 * group + 1]]
    wholes = own[0] // CHUNK
    steps = total // CHUNK - 1
    unroll = 5 if steps % 5 == 0 else 1

    def invert(i, unused):
        place[pos_ref[i]] = i
        return unused

    lax.fori_loop(0, total, invert, 0)
    ones = jnp.ones((CHUNK * BLOCK, HD), jnp.bfloat16)
    for part in range(2):
        for h in range(2):
            q = q_ref[part * BLOCK:(part + 1) * BLOCK, h * HD:(h + 1) * HD]
            q = q.astype(jnp.float32) * SCALE2
            main = q.astype(jnp.bfloat16)
            q_buf[part, h, :, :HD] = main
            q_buf[part, h, :, HD:] = (q - main.astype(jnp.float32)).astype(jnp.bfloat16)

    def load_keys(at):
        keys = jnp.concatenate([key_ref[place[at * CHUNK + b]] for b in range(CHUNK)], axis=0)
        return jnp.concatenate([keys, keys], axis=1)

    def load_values(at):
        values = jnp.concatenate([value_ref[place[at * CHUNK + b]] for b in range(CHUNK)], axis=0)
        return jnp.concatenate([values, ones], axis=1)

    for part in range(2):
        at = own[part] // CHUNK
        keys, values = load_keys(at), load_values(at)
        for h in range(2):
            s = dot(q_buf[part, h], keys, NT)
            ki = lax.broadcasted_iota(jnp.int32, s.shape, 1) + (at * CHUNK - own[part]) * BLOCK
            qi = lax.broadcasted_iota(jnp.int32, s.shape, 0)
            s = jnp.where(ki <= qi, s, LOWEST)
            new = jnp.max(s, axis=1, keepdims=True)
            m_buf[part, h] = jnp.broadcast_to(new, (BLOCK, HD))
            p = jnp.exp2(s - new).astype(jnp.bfloat16)
            acc_buf[part, h] = dot(p, values, NN)

    def place_of(i):
        i = jnp.minimum(i, steps - 1)
        part = (i >= wholes).astype(jnp.int32)
        return part, i - part * wholes

    def score(i, h):
        part, at = place_of(i)
        return dot(q_buf[part, h], load_keys(at), NT)

    s_buf[...] = score(0, 0)

    def step(j, unused):
        ready = s_buf[...]
        for n in range(unroll):
            i = j * unroll + n
            part, at = place_of(i)
            values = load_values(at)
            for h in range(2):
                s = ready
                ready = score(i + h, 1 - h)
                old = m_buf[part, h]
                new = jnp.maximum(old, jnp.max(s, axis=1, keepdims=True))
                m_buf[part, h] = new
                factor = jnp.exp2(old - new)
                p = jnp.exp2(s - new[:, :1]).astype(jnp.bfloat16)
                acc_buf[part, h] = acc_buf[part, h] * factor[:, :1] + dot(p, values, NN)
        s_buf[...] = ready
        return unused

    lax.fori_loop(0, steps // unroll, step, 0)
    for part in range(2):
        for h in range(2):
            acc = acc_buf[part, h]
            o_ref[part * BLOCK:(part + 1) * BLOCK, h * HD:(h + 1) * HD] = (
                acc[:, :HD] / acc[:, HD:]
            ).astype(jnp.bfloat16)

    odd = (group // 2) % 2 == 1
    for h in range(2):
        base = stat_ref[:, h, :]
        best = jnp.max(base, axis=0, keepdims=True)
        share = stat_ref[:, 2 + h, :] * jnp.exp2(base - best)
        share = jnp.concatenate(
            [share, jnp.zeros((HD - chips, HD), jnp.float32)], axis=0
        ).T
        share = jnp.where(odd, share[HD // 2:HD // 2 + fresh], share[:fresh])
        numer = jnp.zeros((fresh, HD), jnp.float32)
        for g in range(chips):
            numer = numer + share[:, g:g + 1] * part_ref[g, :, h * HD:(h + 1) * HD].astype(
                jnp.float32
            )
        denom = jnp.sum(share, axis=1, keepdims=True)
        b_ref[:, h * HD:(h + 1) * HD] = (numer / denom).astype(jnp.bfloat16)


def attend_a(fresh, positions, queries, keys, values, part, stat):
    total = positions.shape[0]
    vmem = pl.BlockSpec(memory_space=pltpu.VMEM)
    return pl.pallas_call(
        functools.partial(a_kernel, fresh),
        out_shape=(
            jax.ShapeDtypeStruct(queries.shape, jnp.bfloat16),
            jax.ShapeDtypeStruct((fresh, 2 * HD), jnp.bfloat16),
        ),
        in_specs=[pl.BlockSpec(memory_space=pltpu.SMEM)] + [vmem] * 5,
        out_specs=[vmem, vmem],
        scratch_shapes=[
            pltpu.VMEM((2, 2, BLOCK, 2 * HD), jnp.bfloat16),
            pltpu.VMEM((BLOCK, CHUNK * BLOCK), jnp.float32),
            pltpu.VMEM((2, 2, BLOCK, HD), jnp.float32),
            pltpu.VMEM((2, 2, BLOCK, 2 * HD), jnp.float32),
            pltpu.SMEM((total,), jnp.int32),
        ],
        compiler_params=pltpu.CompilerParams(vmem_limit_bytes=32 * 2**20),
        cost_estimate=pl.CostEstimate(
            flops=10_000_000_000, bytes_accessed=9_000_000, transcendentals=8_500_000
        ),
        name="attend_a",
    )(positions, queries, keys.reshape(total, -1, HD), values.reshape(total, -1, HD), part, stat)


def shards(
    blocks,
    heads,
    a_query,
    a_key,
    a_value,
    b_query,
    b_key,
    b_value,
    cache_key,
    cache_value,
    a_positions,
    cache_lengths,
):
    *gathered, order = exchange(
        blocks,
        heads,
        cache_lengths,
        a_positions,
        a_key,
        a_value,
        b_query,
        b_key,
        b_value,
        cache_key,
        cache_value,
    )
    return attend_a(b_query.shape[0], order, a_query, *gathered)


def solution(mesh):
    in_specs = (
        P("blk", "tensor"),
        P(("blk", "tensor"), None),
        P(("blk", "tensor"), None),
        P("blk", "tensor"),
        P("blk", None),
        P("blk", None),
        P(("blk", "tensor"), None),
        P(("blk", "tensor"), None),
        P(),
        P(),
    )
    out_specs = (P("blk", "tensor"), P("blk", "tensor"))
    body = functools.partial(shards, mesh.shape["blk"], mesh.shape["tensor"])
    return jax.shard_map(body, mesh=mesh, in_specs=in_specs, out_specs=out_specs, check_vma=False)
```
